512 devices in a mesh: gx: 32 (over y, x), gy: 16 (over z, core).
Axes of the slice: x: 4, y: 8, z: 8, core: 2. Of those that a mesh axis runs over, the one named last changes fastest.
Arguments:
- slip_field: float32 [4096, 3, 128], P(('gy', 'gx')), may hold values from -6 to 6
- positions: float32 [4096, 3, 128], P(('gy', 'gx')), may hold values from -6 to 6
- neighbours: int32 [4096, 8], P(('gy', 'gx')), may hold values from 0 to 255, as said below
- near_counts: int32 [4096], P(('gy', 'gx')), may hold values from 1 to 8, as said below
- cluster_basis: float32 [4096, 16, 3, 128], P(('gy', 'gx')), may hold values from -0.4375 to 0.4375
- transfer: float32 [1022, 16, 16], replicated, may hold values from -1 to 1
- coupling: float32 [1022, 16, 16], replicated, may hold values from -1.5 to 1.5
- prestress: float32 [4096, 3, 128], P(('gy', 'gx')), may hold values from -6 to 6
- normal_stress: float32 [4096, 128], P(('gy', 'gx')), may hold values from 1 to 3
- friction: float32 [4096, 128], P(('gy', 'gx')), may hold values from 0.3 to 0.9
- compliance: float32 [4096, 128], P(('gy', 'gx')), may hold values from 0.1 to 1
- slip_state: int32 [4096, 128], P(('gy', 'gx')), may hold values 0 or 1
- cell_index: int32 [4096, 4, 128], P(('gy', 'gx')), may hold values from 0 to 32767, as said below
- cell_weight: float32 [4096, 4, 128], P(('gy', 'gx')), may hold values from 0.1 to 0.5
- dilation: float32 [4096, 128], P(('gy', 'gx')), may hold values from 1 to 10
- pressure: float32 [256, 2048], P('gx', 'gy'), may hold values from -4 to 4
- mobility: float32 [256, 2048], P('gx', 'gy'), may hold values from 0.05 to 0.24
Outputs:
- final_slip: float32 [4096, 3, 128], P(('gy', 'gx'))
- final_pressure: float32 [256, 2048], P('gx', 'gy')
The draws below stay inside these ranges and needn't reach their ends.
Inputs may be any that keep to these rules, and one draw needn't show every extreme that they name: `neighbours`: entry 0 of a row is the cluster's own number within its subtree; the entries of a row are distinct and lie within 8 clusters of the cluster's own number, counted cyclically within its subtree of 256 clusters. Only the first near_counts[c] entries of a row of neighbours are used; some cluster has exactly 8. `slip_state`: 1 marks an element that slips. `cell_index`: the four cells of an element are band rows r and r + 1 (counted cyclically over the 256 rows) at columns b and b + 1 of the band, in that order: (r, b), (r + 1, b), (r, b + 1), (r + 1, b + 1). For an element of cluster c with j = (c % 256) // 8, both rows lie in (j - 1) * 8 to (j + 2) * 8 - 1, cyclically; both ends are reached in every draw.
All inputs are finite; a program needn't handle non-finite values. No bound on the sum of `slip_state` on one device may be relied on, other than what follows from the above.
Results may differ from the reference program's by a relative error of at most 0.00027.
Values sent between devices are 32-bit elements; how exact they have to be, the bound alone decides.
No kernel may reach another device: no remote copies, remote signals or barrier semaphores. Data moves between devices by JAX's collectives and lax.ppermute only.
A program may use at most 64 MiB of HBM per device.

```python
import math
import jax
import jax.numpy as jnp
from jax import lax

CSIZE = 128
CL_DEV = 8
NB = 8
RANK = 16
IW = 4
FX_DEV = 8
FY_DEV = 128
ITERS = 2
FLOW_STEPS = 2
NODES = 1022
NC = 4096
NFX = 256
NFY = 2048
N_GX = 32
N_GY = 16


def draw_neighbours(key, part):
    subtree_size = CL_DEV * N_GX
    span_size = 2 * CL_DEV
    scores = jax.random.randint(jax.random.fold_in(key, 11), (NC, span_size), 0, 1 << 20) * span_size + jnp.arange(span_size, dtype=jnp.int32)[None, :]
    picked = jnp.argsort(scores, axis=1, stable=True)[:, :NB - 1].astype(jnp.int32)
    shifted = jnp.where(picked < CL_DEV, picked - CL_DEV, picked - CL_DEV + 1)
    local_ids = (jnp.arange(NC, dtype=jnp.int32) % subtree_size)[:, None]
    others = (local_ids + shifted) % subtree_size
    return jnp.concatenate([local_ids, others], axis=1).astype(jnp.int32)


def draw_near_counts(key, part):
    devices = N_GX * N_GY
    heavy_device = jax.random.randint(jax.random.fold_in(key, 21), (devices,), 0, 8) == 0
    lighter = jax.random.randint(jax.random.fold_in(key, 22), (NC,), 1, 4)
    heavier = jnp.minimum(jax.random.randint(jax.random.fold_in(key, 23), (NC,), 5, NB + 4), NB)
    cluster_ids = jnp.arange(NC, dtype=jnp.int32)
    chosen = jnp.where(heavy_device[cluster_ids // CL_DEV], heavier, lighter)
    pinned = jax.random.randint(jax.random.fold_in(key, 24), (), 0, NC)
    return jnp.where(cluster_ids == pinned, NB, chosen).astype(jnp.int32)


def draw_cell_index(key, part):
    band_rows = FX_DEV * N_GX
    cluster_ids = jnp.arange(NC, dtype=jnp.int32)
    column = cluster_ids % (CL_DEV * N_GX) // CL_DEV
    offsets = jax.random.randint(jax.random.fold_in(key, 31), (NC, CSIZE), -FX_DEV, 2 * FX_DEV - 1)
    first_row = (column[:, None] * FX_DEV + offsets) % band_rows
    next_row = (first_row + 1) % band_rows
    first_col = jax.random.randint(jax.random.fold_in(key, 32), (NC, CSIZE), 0, FY_DEV - 1)
    rows = jnp.stack([first_row, next_row, first_row, next_row], axis=1)
    cols = jnp.stack([first_col, first_col, first_col + 1, first_col + 1], axis=1)
    return (rows * FY_DEV + cols).astype(jnp.int32)


def with_ends(entries, stream_key, least, top_value):
    longest = entries.shape.index(max(entries.shape))
    spots = []
    for shift in (0, 1):
        where = [jax.random.randint(jax.random.fold_in(stream_key, axis), (), 0, length) for axis, length in enumerate(entries.shape)]
        where[longest] = (where[longest] + shift) % entries.shape[longest]
        spots.append(tuple(where))
    return entries.at[spots[0]].set(least).at[spots[1]].set(top_value)


def shard_levels(stream_key, dims, pieces, low, top_value):
    factor_of = 1.0
    for axis_at, shards_of in pieces:
        steps = jax.random.uniform(jax.random.fold_in(jax.random.fold_in(stream_key, 6), axis_at), (shards_of,), jnp.float32, low / len(pieces), top_value / len(pieces))
        factor_of = factor_of * jnp.repeat(jnp.exp(steps), dims[axis_at] // shards_of).reshape((-1,) + (1,) * (len(dims) - 1 - axis_at))
    return factor_of


def gaussian(own_key, dims, width, reach, pieces=(), kind=jnp.bfloat16):
    array = width * jax.random.normal(own_key, dims, jnp.float32)
    if pieces:
        array = array * shard_levels(own_key, dims, pieces, -0.22, 0.18)
    return jnp.clip(array, -reach, reach).astype(kind)


def setup_inputs(seed: int = 0) -> dict:
    key_list = jax.random.split(jax.random.key(seed), 18)
    return {
        "slip_field": gaussian(key_list[0], (NC, 3, CSIZE), 1.0, 6.0, ((0, 512),), jnp.float32),
        "positions": gaussian(key_list[1], (NC, 3, CSIZE), 1.0, 6.0, ((0, 512),), jnp.float32),
        "neighbours": draw_neighbours(jax.random.fold_in(key_list[17], 71), 0),
        "near_counts": draw_near_counts(jax.random.fold_in(key_list[17], 71), 0),
        "cluster_basis": gaussian(key_list[4], (NC, RANK, 3, CSIZE), (24 * CL_DEV) ** -0.5, 0.4375, ((0, 512),), jnp.float32),
        "transfer": gaussian(key_list[5], (NODES, RANK, RANK), (2 * RANK) ** -0.5, 1.0, (), jnp.float32),
        "coupling": gaussian(key_list[6], (NODES, RANK, RANK), RANK ** -0.5, 1.5, (), jnp.float32),
        "prestress": gaussian(key_list[7], (NC, 3, CSIZE), 1.0, 6.0, ((0, 512),), jnp.float32),
        "normal_stress": jnp.clip(1.0 + 2.0 * jax.random.uniform(key_list[8], (NC, CSIZE), jnp.float32) ** shard_levels(key_list[8], (NC, CSIZE), ((0, 512),), -0.2, 0.2), 1.0, 3.0),
        "friction": jnp.clip(jnp.exp(math.log(0.9) - 1.0986122 * jax.random.uniform(key_list[9], (NC, CSIZE), jnp.float32) ** shard_levels(key_list[9], (NC, CSIZE), ((0, 512),), -0.2, 0.2)), 0.3, 0.9),
        "compliance": jnp.clip(jnp.exp(math.log(1.0) - 2.3025851 * jax.random.uniform(key_list[10], (NC, CSIZE), jnp.float32) ** shard_levels(key_list[10], (NC, CSIZE), ((0, 512),), -0.2, 0.2)), 0.1, 1.0),
        "slip_state": with_ends((jax.random.randint(key_list[11], (NC, CSIZE), 0, 2) < 1).astype(jnp.int32), jax.random.fold_in(key_list[11], 1), 0, 1),
        "cell_index": draw_cell_index(jax.random.fold_in(key_list[17], 71), 0),
        "cell_weight": jnp.clip(0.1 + 0.4 * jax.random.uniform(key_list[13], (NC, IW, CSIZE), jnp.float32) ** shard_levels(key_list[13], (NC, IW, CSIZE), ((0, 512),), -0.2, 0.2), 0.1, 0.5),
        "dilation": jnp.clip(jnp.exp(math.log(10.0) - 2.3025851 * jax.random.uniform(key_list[14], (NC, CSIZE), jnp.float32) ** shard_levels(key_list[14], (NC, CSIZE), ((0, 512),), -0.2, 0.2)), 1.0, 10.0),
        "pressure": gaussian(key_list[15], (NFX, NFY), 0.5, 4.0, ((0, 32), (1, 16)), jnp.float32),
        "mobility": jnp.clip(jnp.exp(math.log(0.24) - 1.5686159 * jax.random.uniform(key_list[16], (NFX, NFY), jnp.float32) ** shard_levels(key_list[16], (NFX, NFY), ((0, 32), (1, 16)), -0.2, 0.2)), 0.05, 0.24),
    }


HIGHEST = lax.Precision.HIGHEST
KERNEL_SCALE = 0.04
SOFTENING = 0.25

def pair_blocks(targets, sources, slipped):
    offsets = targets[:, :, :, None] - sources[:, :, None, :]
    radius = lax.optimization_barrier(jnp.sum(offsets * offsets, axis=1)) + SOFTENING
    inverse = lax.rsqrt(radius)
    inverse_cube = inverse * inverse * inverse
    projected = lax.optimization_barrier(jnp.sum(offsets * slipped[:, :, None, :], axis=1))
    direct = lax.optimization_barrier(jnp.sum(inverse[:, None] * slipped[:, :, None, :], axis=3))
    dyadic = lax.optimization_barrier(jnp.sum(offsets * (projected * inverse_cube)[:, None], axis=3))
    return KERNEL_SCALE * (direct + dyadic)

def reference(slip_field, positions, neighbours, near_counts, cluster_basis, transfer, coupling, prestress, normal_stress, friction, compliance, slip_state, cell_index, cell_weight, dilation, pressure, mobility):
    subtree_size = CL_DEV * N_GX
    devices = N_GX * N_GY
    levels = devices.bit_length() - 1
    cluster_ids = jnp.arange(NC, dtype=jnp.int32)
    source_ids = (cluster_ids // subtree_size * subtree_size)[:, None] + neighbours
    slot_ids = jnp.arange(NB, dtype=jnp.int32)
    active = slot_ids[None, :] < near_counts[:, None]
    band_size = NFX * FY_DEV
    global_cells = (cluster_ids // subtree_size)[:, None, None] * band_size + cell_index
    state_mask = slip_state.astype(jnp.float32)
    for outer_step in range(ITERS):

        def near_cluster(packed):
            own_id, source_row, active_row = packed
            targets = jnp.broadcast_to(positions[own_id], (NB, 3, CSIZE))
            blocks = pair_blocks(targets, positions[source_row], slip_field[source_row])
            return lax.optimization_barrier(jnp.sum(jnp.where(active_row[:, None, None], blocks, 0.0), axis=0))
        near_part = lax.map(near_cluster, (cluster_ids, source_ids, active))
        moments = jnp.einsum('ckia,cia->ck', cluster_basis, slip_field, precision=HIGHEST)
        moments = moments.reshape(devices, CL_DEV, RANK).sum(axis=1)
        tier_moments = [moments]
        for tier_level in range(levels):
            node_count = devices >> tier_level
            node_base = 2 * devices - 2 * node_count
            lifted = jnp.einsum('nmk,nm->nk', transfer[node_base:node_base + node_count], tier_moments[-1], precision=HIGHEST)
            tier_moments.append(lifted[0::2] + lifted[1::2])
        incoming = jnp.zeros((1, RANK), jnp.float32)
        for tier_level in reversed(range(levels)):
            node_count = devices >> tier_level
            node_base = 2 * devices - 2 * node_count
            node_ids = jnp.arange(node_count, dtype=jnp.int32)
            parent_field = incoming[node_ids // 2]
            sibling = tier_moments[tier_level][jnp.bitwise_xor(node_ids, 1)]
            incoming = jnp.einsum('nmk,nk->nm', transfer[node_base:node_base + node_count], parent_field, precision=HIGHEST) + jnp.einsum('nmk,nk->nm', coupling[node_base:node_base + node_count], sibling, precision=HIGHEST)
        far_part = jnp.einsum('ckia,ck->cia', cluster_basis, incoming[cluster_ids // CL_DEV], precision=HIGHEST)
        pressure_bands = pressure.reshape(NFX, N_GY, FY_DEV).transpose(1, 0, 2).reshape(-1)
        at_elements = lax.optimization_barrier(jnp.sum(cell_weight * pressure_bands[global_cells], axis=1))
        stress = prestress - (near_part + far_part)
        effective = normal_stress - at_elements
        magnitude = jnp.sqrt(lax.optimization_barrier(jnp.sum(stress * stress, axis=1)) + 1.0)
        factor = jnp.maximum(1.0 - friction * effective / magnitude, 0.0)
        step_slip = (state_mask * compliance * factor)[:, None, :] * stress
        slip_field = slip_field + step_slip
        dilated = dilation * lax.optimization_barrier(jnp.sum(step_slip * step_slip, axis=1))
        loaded = jax.ops.segment_sum((cell_weight * dilated[:, None, :]).reshape(-1), global_cells.reshape(-1), num_segments=N_GY * band_size)
        source = loaded.reshape(N_GY, NFX, FY_DEV).transpose(1, 0, 2).reshape(NFX, NFY)
        pressure = pressure + source
        for flow_step in range(FLOW_STEPS):
            padded = jnp.pad(pressure, 1)
            beside_all = padded[2:, 1:-1] + padded[:-2, 1:-1] + padded[1:-1, 2:] + padded[1:-1, :-2]
            pressure = pressure + mobility * (beside_all - 4.0 * pressure)
    return (slip_field, pressure)
```

```python
import jax
import jax.numpy as jnp
from jax import lax
from jax.experimental import pallas as pl
from jax.experimental.pallas import tpu as pltpu
from jax.sharding import PartitionSpec as P

HI = lax.Precision.HIGHEST
F32 = jnp.float32
BF16 = jnp.bfloat16
SCALE = 0.04
SOFT = 0.25
LV = 9
RK = 16
GX_BITS = 5
WIDE = 18
NARROW = 10
HALO = 10

NN = (((1,), (0,)), ((), ()))
NT = (((1,), (1,)), ((), ()))
TN = (((0,), (0,)), ((), ()))


def dot(a, b, dims=NN, precision=HI):
    return lax.dot_general(a, b, dims, precision=precision, preferred_element_type=F32)


def iota(shape, dim):
    return lax.broadcasted_iota(jnp.int32, shape, dim)


def thirds(x):
    hi = x.astype(BF16)
    rest = x - hi.astype(F32)
    mid = rest.astype(BF16)
    low = (rest - mid.astype(F32)).astype(BF16)
    return jnp.concatenate([hi, mid, low], axis=0)


def call(kernel, outs, args, scratch=(), smem=0, flops=0):
    specs = [pl.BlockSpec(memory_space=pltpu.SMEM)] * smem
    specs += [pl.BlockSpec(memory_space=pltpu.VMEM)] * (len(args) - smem)
    return pl.pallas_call(
        kernel,
        out_shape=[jax.ShapeDtypeStruct(s, d) for s, d in outs],
        in_specs=specs,
        out_specs=[pl.BlockSpec(memory_space=pltpu.VMEM)] * len(outs),
        scratch_shapes=list(scratch),
        compiler_params=pltpu.CompilerParams(vmem_limit_bytes=32 * 1024 * 1024),
        cost_estimate=pl.CostEstimate(flops=flops, bytes_accessed=1 << 20, transcendentals=0),
    )(*args)


def project(basis_ref, slip_rows, g_ref):
    total = jnp.zeros((RK, 128), F32)
    for c in range(8):
        for i in range(3):
            total += basis_ref[c, i] * slip_rows(i, c)
    moment = dot(jnp.ones((8, 128), F32), total, NT)
    return dot(moment, g_ref[0:128, :], NT), dot(moment, g_ref[128:256, :], NT)


def setup_kernel(
    place, slip, basis, transfer, coupling, pressure, mobility, g_out, h_out, tile_out
):
    flat = place[2]
    nodes = transfer.shape[1]
    spot = iota((nodes, 256), 0)
    level = iota((nodes, 256), 1) // RK
    first = 1024 - jnp.right_shift(jnp.full(level.shape, 1024, jnp.int32), level)
    wanted = first + jnp.right_shift(jnp.full(level.shape, 0, jnp.int32) + flat, level)
    pick = jnp.where((spot == wanted) & (level < LV), 1.0, 0.0).astype(F32)
    mine = (iota((256, 256), 1) % RK) == (iota((256, 256), 0) // RK)

    def path_matrices(table):
        spread = jnp.where(mine, dot(table[...], pick), 0.0)
        return jnp.sum(spread.reshape(RK, RK, 256), axis=0)

    lifts = path_matrices(transfer)
    across = path_matrices(coupling)
    eye = jnp.where(iota((RK, RK), 0) == iota((RK, RK), 1), 1.0, 0.0).astype(F32)
    g_out[...] = jnp.zeros(g_out.shape, F32)
    h_out[...] = jnp.zeros(h_out.shape, F32)
    chain = eye
    for l in range(LV):
        g_out[l * RK : (l + 1) * RK, :] = chain
        h_out[l * RK : (l + 1) * RK, :] = dot(across[:, l * RK : (l + 1) * RK], chain)
        if l + 1 < LV:
            chain = dot(lifts[:, l * RK : (l + 1) * RK], chain)
    low, high = project(basis, lambda i, c: slip[i, c : c + 1, :], g_out)
    tile_out[...] = jnp.zeros(tile_out.shape, F32)
    tile_out[0:8, :] = pressure[...]
    tile_out[8:16, :] = mobility[...]
    tile_out[18:19, :] = low[0:1]
    tile_out[19:20, :] = high[0:1]


def cells_kernel(row_in, col_in, weight, pick_out, weight_out):
    for c in range(8):
        lanes = slice(c * 128, (c + 1) * 128)
        row = row_in[c : c + 1, :]
        col = col_in[c : c + 1, :]
        pick_out[:, lanes] = jnp.where(iota((128, 128), 0) == col, 1.0, 0.0).astype(BF16)
        at = iota((24, 128), 0)
        for side in range(2):
            weight_out[side * 24 : side * 24 + 24, lanes] = jnp.where(
                at == row, weight[2 * side, c : c + 1, :], 0.0
            ) + jnp.where(at == row + 1, weight[2 * side + 1, c : c + 1, :], 0.0)


def near_kernel(counts, slots, points, slips, near_out, target, total):
    ones = jnp.ones((128, 128), F32)
    diagonal = iota((128, 128), 0) == iota((128, 128), 1)
    for c in range(8):
        for i in range(3):
            target[i] = jnp.transpose(jnp.broadcast_to(points[1, i, c : c + 1, :], (128, 128)))
        total[...] = jnp.zeros(total.shape, F32)

        def one_source(k, _):
            slot = slots[c, k]
            block = slot // 8
            row = pl.ds(slot % 8, 1)
            y = [points[block, i, row, :] for i in range(3)]
            s = [slips[block, i, row, :] for i in range(3)]
            for part in range(8):
                rows = slice(part * 16, part * 16 + 16)
                r = [target[i, rows, :] - y[i] for i in range(3)]
                inverse = lax.rsqrt(r[0] * r[0] + r[1] * r[1] + r[2] * r[2] + SOFT)
                along = (r[0] * s[0] + r[1] * s[1] + r[2] * s[2]) * (inverse * inverse)
                for i in range(3):
                    total[i, rows, :] += inverse * (s[i] + along * r[i])
            return 0

        lax.fori_loop(0, counts[c], one_source, 0)
        for i in range(3):
            summed = dot(total[i], ones)
            near_out[i, c : c + 1, :] = SCALE * jnp.sum(
                jnp.where(diagonal, summed, 0.0), axis=0, keepdims=True
            )


def pick_edges(window):
    row, lane = iota((8, 128), 0), iota((8, 128), 1)
    wanted = jnp.where(row < 2, row, row + 124)
    pick = jnp.where((lane == wanted) & (row < 4), 1.0, 0.0).astype(F32)
    return dot(pick, window, NT)


def spread_edges(edges, width):
    row, lane = iota((8, 128), 0), iota((8, 128), 1)
    wanted = jnp.where(row < 2, row, row + 124)
    pick = jnp.where((lane == wanted) & (row < 4), 1.0, 0.0).astype(F32)
    return dot(edges[:, 0:32], pick, TN)


def sum_over_row(place, received):
    j = place[0]
    row, lane = iota((8, 128), 0), iota((8, 128), 1)
    level = lane // RK + jnp.where(row == 3, 8, 0)
    own = jnp.right_shift(jnp.zeros((8, 128), jnp.int32) + j, level)
    total = jnp.zeros((8, 128), F32)
    for p in range(received.shape[0]):
        theirs = jnp.right_shift(jnp.full((8, 128), p, jnp.int32), level)
        used = (level >= GX_BITS) | (theirs == jnp.bitwise_xor(own, 1))
        total += jnp.where(used, received[p, 16:24, :], 0.0)
    return total


def first_kernel(place, received, pressure_out, mobility_out, tile_out):
    j = place[0]
    peers = received.shape[0]
    pressure_out[...] = jnp.zeros(pressure_out.shape, F32)
    mobility_out[...] = jnp.zeros(mobility_out.shape, F32)
    for out, at in ((pressure_out, 0), (mobility_out, 8)):
        for off in (-1, 0, 1):
            p = lax.rem(j + off + peers, peers)
            out[HALO + 8 * off : HALO + 8 * off + 8, :] = received[p, at : at + 8, :]
        p = lax.rem(j - 2 + peers, peers)
        out[0:2, :] = received[p, at + 6 : at + 8, :]
        p = lax.rem(j + 2, peers)
        out[26:28, :] = received[p, at : at + 2, :]
    sums = sum_over_row(place, received)
    tile_out[...] = jnp.zeros(tile_out.shape, F32)
    edges = pick_edges(mobility_out[...])
    tile_out[4:5, :] = sums[2:3]
    tile_out[5:6, :] = sums[3:4]
    tile_out[0:4, 0:32] = edges[0:4]


def add_sources(place, received, loaded, window, rows):
    j = place[0]
    peers = received.shape[0]
    window[2:26, :] += loaded[...]
    for off in range(1, 4):
        kept = rows - 8 * (off - 1)
        if kept <= 0:
            continue
        p = lax.rem(j + off, peers)
        at = HALO + 8 * (off - 1)
        window[at : at + kept, :] += received[p, 0:kept, :]
        p = lax.rem(j - off + peers, peers)
        at = HALO + 8 - rows
        window[at : at + kept, :] += received[p, rows - kept : rows, :]


def between_kernel(place, received, loaded, pressure, window_out, tile_out):
    window_out[...] = pressure[...]
    add_sources(place, received, loaded, window_out, WIDE)
    sums = sum_over_row(place, received)
    tile_out[...] = jnp.zeros(tile_out.shape, F32)
    edges = pick_edges(window_out[...])
    tile_out[0:4, 0:32] = edges[0:4]
    tile_out[4:5, :] = sums[2:3]
    tile_out[5:6, :] = sums[3:4]


def last_kernel(place, received, loaded, pressure, window_out, tile_out):
    window_out[...] = pressure[...]
    add_sources(place, received, loaded, window_out, NARROW)
    tile_out[...] = jnp.zeros(tile_out.shape, F32)
    tile_out[0:4, 0:32] = pick_edges(window_out[...])[0:4]


def beside(place, left, right):
    g = place[1]
    row = iota((8, 128), 0)
    edges = jnp.where((row < 2) & (g < place[3] - 1), right, 0.0)
    edges += jnp.where((row >= 2) & (row < 4) & (g > 0), left, 0.0)
    return spread_edges(edges, 128)


def flow(place, window, window_side, mobility, mobility_side):
    j = place[0]
    p = jnp.concatenate([window, window_side], axis=1)
    lane = iota((32, 128), 1)
    m_side = jnp.where((lane == 0) | (lane == 127), mobility_side, 0.0)
    m = jnp.concatenate([mobility, m_side], axis=1)
    rows = place[4]
    row = lax.rem(iota((32, 256), 0) + (j * 8 - HALO + rows), jnp.full((32, 256), 0, jnp.int32) + rows)
    for step in range(2):
        up = jnp.where(row == 0, 0.0, pltpu.roll(p, 1, 0))
        down = jnp.where(row == rows - 1, 0.0, pltpu.roll(p, 31, 0))
        sides = pltpu.roll(p, 1, 1) + pltpu.roll(p, 255, 1)
        p = p + m * (up + down + sides - 4.0 * p)
    return p[:, 0:128]


def update(place, received, tile, near, refs, window, slip_out, loaded_out):
    (slip, prestress, basis, normal, friction, compliance, state, dilation, pick, weight, h) = refs
    g = place[1]
    row, lane = iota((8, 128), 0), iota((8, 128), 1)
    level = lane // RK + jnp.where(row == 5, 8, 0)
    bit = jnp.maximum(level - GX_BITS, 0)
    own = jnp.right_shift(jnp.zeros((8, 128), jnp.int32) + g, bit)
    total = jnp.where((level < GX_BITS) & (row == 4), tile[...], 0.0)
    within = (level >= GX_BITS) & (level < LV) & ((row == 4) | (row == 5))
    for p in range(received.shape[0]):
        theirs = jnp.right_shift(jnp.full((8, 128), p, jnp.int32), bit)
        total += jnp.where(within & (theirs == jnp.bitwise_xor(own, 1)), received[p], 0.0)
    parts = jnp.where(iota((8, RK), 0) == 4, dot(total, h[0:128, :]), 0.0)
    parts += jnp.where(iota((8, RK), 0) == 5, dot(total, h[128:256, :]), 0.0)
    incoming = dot(parts, jnp.ones((8, 128), F32), TN)

    cells = window[2:26, :]
    both = jnp.concatenate([cells, pltpu.roll(cells, 127, 1)], axis=0)
    split = thirds(both)
    found = dot(split, pick[...], NN, None)
    found = (found[0:48] + found[48:96] + found[96:144]) * weight[...]
    at_row = jnp.sum(found, axis=0, keepdims=True)

    for c in range(8):
        for i in range(3):
            far = jnp.sum(basis[c, i] * incoming, axis=0, keepdims=True)
            slip_out[i, c : c + 1, :] = far
    at_elements = jnp.concatenate([at_row[:, c * 128 : (c + 1) * 128] for c in range(8)], axis=0)
    stress = [prestress[i] - (near[i] + slip_out[i]) for i in range(3)]
    effective = normal[...] - at_elements
    magnitude = jnp.sqrt(stress[0] * stress[0] + stress[1] * stress[1] + stress[2] * stress[2] + 1.0)
    factor = jnp.maximum(1.0 - friction[...] * effective / magnitude, 0.0)
    scaled = state[...].astype(F32) * compliance[...] * factor
    steps = [scaled * stress[i] for i in range(3)]
    for i in range(3):
        slip_out[i] = slip[i] + steps[i]
    dilated = dilation[...] * (steps[0] * steps[0] + steps[1] * steps[1] + steps[2] * steps[2])
    dilated_row = jnp.concatenate([dilated[c : c + 1, :] for c in range(8)], axis=1)
    spread = dot(thirds(weight[...] * dilated_row), pick[...], NT, None)
    spread = spread[0:48] + spread[48:96] + spread[96:144]
    loaded_out[...] = spread[0:24] + pltpu.roll(spread[24:48], 1, 1)


def send_tiles(ahead_out, behind_out, loaded, rows):
    ahead_out[...] = jnp.zeros(ahead_out.shape, F32)
    behind_out[...] = jnp.zeros(behind_out.shape, F32)
    ahead_out[0:rows, :] = loaded[0:rows, :]
    behind_out[0:rows, :] = loaded[24 - rows : 24, :]


def first_update_kernel(place, received, tile, near, *refs):
    refs, (window, lifts), outs = refs[:11], refs[11:13], refs[13:]
    slip_out, loaded_out, ahead_out, behind_out = outs
    update(place, received, tile, near, refs, window, slip_out, loaded_out)
    low, high = project(refs[2], lambda i, c: slip_out[i, c : c + 1, :], lifts)
    send_tiles(ahead_out, behind_out, loaded_out, WIDE)
    for out in (ahead_out, behind_out):
        out[18:19, :] = low[0:1]
        out[19:20, :] = high[0:1]


def second_update_kernel(place, received, tile, near, *refs):
    refs, (window, mobility, mobility_side), outs = refs[:11], refs[11:14], refs[14:]
    slip_out, loaded_out, ahead_out, behind_out, window_out = outs
    g = place[1]
    left = received[jnp.maximum(g - 1, 0)]
    right = received[jnp.minimum(g + 1, received.shape[0] - 1)]
    side = beside(place, left, right)
    window_out[...] = flow(place, window[...], side, mobility[...], mobility_side[...])
    update(place, received, tile, near, refs, window_out, slip_out, loaded_out)
    send_tiles(ahead_out, behind_out, loaded_out, NARROW)


def side_kernel(place, received, side_out):
    g = place[1]
    left = received[jnp.maximum(g - 1, 0)]
    right = received[jnp.minimum(g + 1, received.shape[0] - 1)]
    side_out[...] = beside(place, left, right)


def final_kernel(place, window, left, right, mobility, mobility_side, out):
    side = beside(place, left[...], right[...])
    done = flow(place, window[...], side, mobility[...], mobility_side[...])
    out[...] = done[HALO : HALO + 8, :]


def shift(x, axis, steps):
    n = lax.axis_size(axis)
    return lax.ppermute(x, axis, [(i, (i + steps) % n) for i in range(n)])


def shards(
    slip_field,
    positions,
    neighbours,
    near_counts,
    cluster_basis,
    transfer,
    coupling,
    prestress,
    normal_stress,
    friction,
    compliance,
    slip_state,
    cell_index,
    cell_weight,
    dilation,
    pressure,
    mobility,
):
    nx, ny = lax.axis_size("gx"), lax.axis_size("gy")
    j, g = lax.axis_index("gx"), lax.axis_index("gy")
    rows = 8 * nx
    place = jnp.stack([j, g, g * nx + j, jnp.int32(ny), jnp.int32(rows)]).astype(jnp.int32)
    slip = slip_field.transpose(1, 0, 2)
    points = positions.transpose(1, 0, 2)
    strained = prestress.transpose(1, 0, 2)
    basis = cluster_basis.transpose(0, 2, 1, 3)
    lift_table = transfer.transpose(1, 2, 0).reshape(RK * RK, -1)
    cross_table = coupling.transpose(1, 2, 0).reshape(RK * RK, -1)
    slots = (neighbours - j * 8 + 8 + rows) % rows
    first_cell = cell_index[:, 0, :]
    cell_row = (first_cell // 128 - j * 8 + 8 + rows) % rows
    cell_col = first_cell % 128
    weights = cell_weight.transpose(1, 0, 2)
    ahead_of = (j - jnp.arange(nx, dtype=jnp.int32)) % nx < nx // 2

    both = jnp.concatenate([points, slip], axis=0)
    from_low = shift(both, "gx", 1)
    from_high = shift(both, "gx", -1)
    all_points = jnp.stack([from_low[0:3], points, from_high[0:3]])
    all_slips = jnp.stack([from_low[3:6], slip, from_high[3:6]])

    g_mat, h_mat, tile = call(
        setup_kernel,
        [((256, RK), F32), ((256, RK), F32), ((24, 128), F32)],
        [place, slip, basis, lift_table, cross_table, pressure, mobility],
        smem=1,
    )
    received = lax.all_to_all(jnp.broadcast_to(tile[None], (nx, 24, 128)), "gx", 0, 0, tiled=True)
    pick, weight = call(
        cells_kernel,
        [((128, 1024), BF16), ((48, 1024), F32)],
        [cell_row, cell_col, weights],
        flops=1 << 20,
    )
    window, mobility_window, tile = call(
        first_kernel,
        [((32, 128), F32), ((32, 128), F32), ((8, 128), F32)],
        [place, received],
        smem=1,
    )
    mobility_side = None

    for outer_step in range(2):
        received = lax.all_to_all(
            jnp.broadcast_to(tile[None], (ny, 8, 128)), "gy", 0, 0, tiled=True
        )
        (near,) = call(
            near_kernel,
            [((3, 8, 128), F32)],
            [near_counts, slots, all_points, all_slips],
            scratch=[pltpu.VMEM((3, 128, 128), F32), pltpu.VMEM((3, 128, 128), F32)],
            smem=2,
            flops=1 << 30,
        )
        common = [slip, strained, basis, normal_stress, friction, compliance, slip_state]
        common += [dilation, pick, weight, h_mat]
        if outer_step == 0:
            (mobility_side,) = call(side_kernel, [((32, 128), F32)], [place, received], smem=1)
            slip, loaded, ahead, behind = call(
                first_update_kernel,
                [((3, 8, 128), F32), ((24, 128), F32), ((24, 128), F32), ((24, 128), F32)],
                [place, received, tile, near, *common, window, g_mat],
                smem=1,
            )
        else:
            slip, loaded, ahead, behind, window = call(
                second_update_kernel,
                [
                    ((3, 8, 128), F32),
                    ((24, 128), F32),
                    ((16, 128), F32),
                    ((16, 128), F32),
                    ((32, 128), F32),
                ],
                [place, received, tile, near, *common, window, mobility_window, mobility_side],
                smem=1,
            )
        sent = jnp.where(ahead_of[:, None, None], ahead[None], behind[None])
        received = lax.all_to_all(sent, "gx", 0, 0, tiled=True)
        if outer_step == 0:
            from_low = shift(slip, "gx", 1)
            from_high = shift(slip, "gx", -1)
            all_slips = jnp.stack([from_low, slip, from_high])
        window, tile = call(
            between_kernel if outer_step == 0 else last_kernel,
            [((32, 128), F32), ((8, 128), F32)],
            [place, received, loaded, window],
            smem=1,
        )
    left = shift(tile, "gy", 1)
    right = shift(tile, "gy", -1)
    (final_pressure,) = call(
        final_kernel,
        [((8, 128), F32)],
        [place, window, left, right, mobility_window, mobility_side],
        smem=1,
    )
    return (slip.transpose(1, 0, 2), final_pressure)


def solution(mesh):
    split = ("gy", "gx")
    in_specs = (
        P(split, None, None),
        P(split, None, None),
        P(split, None),
        P(split),
        P(split, None, None, None),
        P(),
        P(),
        P(split, None, None),
        P(split, None),
        P(split, None),
        P(split, None),
        P(split, None),
        P(split, None, None),
        P(split, None, None),
        P(split, None),
        P("gx", "gy"),
        P("gx", "gy"),
    )
    out_specs = (P(split, None, None), P("gx", "gy"))
    return jax.shard_map(shards, mesh=mesh, in_specs=in_specs, out_specs=out_specs, check_vma=False)
```

```python
import jax
import jax.numpy as jnp
from jax import lax
from jax.experimental import pallas as pl
from jax.experimental.pallas import tpu as pltpu
from jax.sharding import PartitionSpec as P

HI = lax.Precision.HIGHEST
F32 = jnp.float32
BF16 = jnp.bfloat16
SCALE = 0.04
SOFT = 0.25
LV = 9
RK = 16
GX_BITS = 5
HALO = 10

NN = (((1,), (0,)), ((), ()))
NT = (((1,), (1,)), ((), ()))
TN = (((0,), (0,)), ((), ()))


def dot(a, b, dims=NN, precision=HI):
    return lax.dot_general(a, b, dims, precision=precision, preferred_element_type=F32)


def iota(shape, dim):
    return lax.broadcasted_iota(jnp.int32, shape, dim)


def thirds(x):
    hi = x.astype(BF16)
    rest = x - hi.astype(F32)
    mid = rest.astype(BF16)
    low = (rest - mid.astype(F32)).astype(BF16)
    return jnp.concatenate([hi, mid, low], axis=0)


def call(kernel, outs, args, scratch=(), smem=0, far=0, flops=0, room=32):
    specs = [pl.BlockSpec(memory_space=pltpu.SMEM)] * smem
    specs += [pl.BlockSpec(memory_space=pl.ANY)] * far
    specs += [pl.BlockSpec(memory_space=pltpu.VMEM)] * (len(args) - smem - far)
    return pl.pallas_call(
        kernel,
        out_shape=[jax.ShapeDtypeStruct(s, d) for s, d in outs],
        in_specs=specs,
        out_specs=[pl.BlockSpec(memory_space=pltpu.VMEM)] * len(outs),
        scratch_shapes=list(scratch),
        compiler_params=pltpu.CompilerParams(vmem_limit_bytes=room * 1024 * 1024),
        cost_estimate=pl.CostEstimate(flops=flops, bytes_accessed=1 << 20, transcendentals=0),
    )(*args)


def project(basis_ref, slip_rows, g_ref):
    total = jnp.zeros((RK, 128), F32)
    for c in range(8):
        for i in range(3):
            total += basis_ref[c, i] * slip_rows(i, c)
    moment = dot(jnp.ones((8, 128), F32), total, NT)
    return dot(moment, g_ref[0:128, :], NT), dot(moment, g_ref[128:256, :], NT)


def setup_kernel(
    place,
    transfer,
    coupling,
    transfer_end,
    coupling_end,
    slip,
    basis,
    pressure,
    mobility,
    g_out,
    h_out,
    sent,
    held,
    sems,
):
    flat = place[2]
    blocks = [pl.multiple_of(flat // 128 * 128, 128), pl.multiple_of(512 + flat // 256 * 128, 128)]
    blocks += [768, 896]
    copies = []
    for t, table in enumerate((transfer, coupling)):
        for b, start in enumerate(blocks[:3]):
            copies.append(
                pltpu.make_async_copy(
                    table.at[:, pl.ds(start, 128)], held.at[t, b], sems.at[t * 3 + b]
                )
            )
            copies[-1].start()
    total = jnp.zeros((RK, 128), F32)
    for c in range(8):
        for i in range(3):
            total += basis[c, i] * slip[i, c : c + 1, :]
    moment = dot(jnp.ones((8, 128), F32), total, NT)

    shape = (128, 256)
    level = iota(shape, 1) // RK
    first = 1024 - jnp.right_shift(jnp.full(shape, 1024, jnp.int32), level)
    wanted = first + jnp.right_shift(jnp.zeros(shape, jnp.int32) + flat, level)
    picks = []
    for b, start in enumerate(blocks):
        used = (level == b) if b < 3 else (level >= 3) & (level < LV)
        picks.append(jnp.where((iota(shape, 0) + start == wanted) & used, 1.0, 0.0).astype(BF16))
    mine = (iota((256, 256), 1) % RK) == (iota((256, 256), 0) // RK)
    for copy in copies:
        copy.wait()

    def path_matrices(t, end):
        spread = jnp.zeros((768, 256), F32)
        for b in range(4):
            block = held[t, b] if b < 3 else end[...]
            spread += dot(thirds(block), picks[b], NN, None)
        spread = spread[0:256] + spread[256:512] + spread[512:768]
        return jnp.sum(jnp.where(mine, spread, 0.0).reshape(RK, RK, 256), axis=0)

    lifts = path_matrices(0, transfer_end)
    across = path_matrices(1, coupling_end)
    eye = jnp.where(iota((RK, RK), 0) == iota((RK, RK), 1), 1.0, 0.0).astype(F32)
    g_out[...] = jnp.zeros(g_out.shape, F32)
    h_out[...] = jnp.zeros(h_out.shape, F32)
    chain = eye
    for l in range(LV):
        g_out[l * RK : (l + 1) * RK, :] = chain
        h_out[l * RK : (l + 1) * RK, :] = dot(across[:, l * RK : (l + 1) * RK], chain)
        if l + 1 < LV:
            chain = dot(lifts[:, l * RK : (l + 1) * RK], chain)
    low = dot(moment, g_out[0:128, :], NT)
    high = dot(moment, g_out[128:256, :], NT)
    row = iota((8, 128), 0)
    tile = jnp.where(row == 6, low, jnp.where(row == 7, high, 0.0))
    sent[0] = tile
    sent[0, 0:2, :] = pressure[0:2, :]
    sent[0, 2:4, :] = pressure[6:8, :]
    sent[0, 4:5, :] = mobility[0:1, :]
    sent[0, 5:6, :] = mobility[7:8, :]
    for p in range(1, sent.shape[0]):
        sent[p] = sent[0]


def cells_kernel(row_in, col_in, weight, pick_out, weight_out):
    for c in range(8):
        lanes = slice(c * 128, (c + 1) * 128)
        row = row_in[c : c + 1, :]
        col = col_in[c : c + 1, :]
        pick_out[:, lanes] = jnp.where(iota((128, 128), 0) == col, 1.0, 0.0).astype(BF16)
        at = iota((24, 128), 0)
        for side in range(2):
            weight_out[side * 24 : side * 24 + 24, lanes] = jnp.where(
                at == row, weight[2 * side, c : c + 1, :], 0.0
            ) + jnp.where(at == row + 1, weight[2 * side + 1, c : c + 1, :], 0.0)


def near_kernel(counts, slots, own_points, low_points, high_points, own, low, high, near_out, points, slips, target, total):
    ones = jnp.ones((128, 128), BF16)
    diagonal = iota((128, 128), 0) == iota((128, 128), 1)
    for b, (p, s) in enumerate(((low_points, low), (own_points, own), (high_points, high))):
        for i in range(3):
            points[b, i] = p[i]
            slips[b, i] = s[i]
    for c in range(8):
        for i in range(3):
            wide = jnp.where(diagonal, own_points[i, c : c + 1, :], 0.0)
            wide = dot(thirds(wide), ones, NN, None)
            target[i] = wide[0:128] + wide[128:256] + wide[256:384]
        total[...] = jnp.zeros(total.shape, F32)

        def one_source(k, _):
            slot = slots[c, k]
            block = slot // 8
            row = pl.ds(slot % 8, 1)
            y = [points[block, i, row, :] for i in range(3)]
            s = [slips[block, i, row, :] for i in range(3)]
            for part in range(8):
                rows = slice(part * 16, part * 16 + 16)
                r = [target[i, rows, :] - y[i] for i in range(3)]
                inverse = lax.rsqrt(r[0] * r[0] + r[1] * r[1] + r[2] * r[2] + SOFT)
                along = (r[0] * s[0] + r[1] * s[1] + r[2] * s[2]) * (inverse * inverse)
                for i in range(3):
                    total[i, rows, :] += inverse * (s[i] + along * r[i])
            return 0

        lax.fori_loop(0, counts[c], one_source, 0)
        for i in range(3):
            summed = dot(thirds(total[i]), ones, NN, None)
            summed = summed[0:128] + summed[128:256] + summed[256:384]
            near_out[i, c : c + 1, :] = SCALE * jnp.sum(
                jnp.where(diagonal, summed, 0.0), axis=0, keepdims=True
            )


def pick_edges(window):
    row, lane = iota((8, 128), 0), iota((8, 128), 1)
    wanted = jnp.where(row < 2, row, row + 124)
    pick = jnp.where((lane == wanted) & (row < 4), 1.0, 0.0).astype(F32)
    return dot(pick, window, NT)


def spread_edges(edges, width):
    row, lane = iota((8, 128), 0), iota((8, 128), 1)
    wanted = jnp.where(row < 2, row, row + 124)
    pick = jnp.where((lane == wanted) & (row < 4), 1.0, 0.0).astype(F32)
    return dot(edges[:, 0:32], pick, TN)


def sum_over_row(place, received, at, first):
    j = place[0]
    row, lane = iota((8, 128), 0), iota((8, 128), 1)
    level = lane // RK + jnp.where(row == first + 1, 8, 0)
    own = jnp.right_shift(jnp.zeros((8, 128), jnp.int32) + j, level)
    total = jnp.zeros((8, 128), F32)
    for p in range(received.shape[0]):
        theirs = jnp.right_shift(jnp.full((8, 128), p, jnp.int32), level)
        used = (level >= GX_BITS) | (theirs == jnp.bitwise_xor(own, 1))
        total += jnp.where(used, received[p, at : at + 8, :], 0.0)
    return total


def copies_of(tile, sent):
    for p in range(sent.shape[0]):
        sent[p] = tile[...]


def first_kernel(place, received, low, high, pressure, mobility, pressure_out, mobility_out, tile_out, sent):
    j = place[0]
    peers = received.shape[0]
    before = lax.rem(j - 2 + peers, peers)
    after = lax.rem(j + 2, peers)
    pressure_out[...] = jnp.zeros(pressure_out.shape, F32)
    mobility_out[...] = jnp.zeros(mobility_out.shape, F32)
    pressure_out[0:2, :] = received[before, 2:4, :]
    pressure_out[2:10, :] = low[6]
    pressure_out[10:18, :] = pressure[...]
    pressure_out[18:26, :] = high[6]
    pressure_out[26:28, :] = received[after, 0:2, :]
    mobility_out[1:2, :] = received[before, 5:6, :]
    mobility_out[2:10, :] = low[7]
    mobility_out[10:18, :] = mobility[...]
    mobility_out[18:26, :] = high[7]
    mobility_out[26:27, :] = received[after, 4:5, :]
    sums = sum_over_row(place, received, 0, 6)
    tile_out[...] = jnp.zeros(tile_out.shape, F32)
    edges = pick_edges(mobility_out[...])
    tile_out[4:6, :] = sums[6:8]
    tile_out[0:4, 0:32] = edges[0:4]
    copies_of(tile_out, sent)


def between_kernel(place, received, low, high, loaded, pressure, window, tile_out, sent):
    j = place[0]
    peers = received.shape[0]
    window[...] = pressure[...]
    window[2:26, :] += loaded[...]
    for i, at, size in ((3, 0, 8), (4, 8, 8), (5, 16, 2)):
        window[at : at + size, :] += low[i, 0:size, :]
        window[at + 10 : at + 10 + size, :] += high[i, 0:size, :]
    window[18:28, :] += received[lax.rem(j + 2, peers), 0:10, :]
    window[0:10, :] += received[lax.rem(j - 2 + peers, peers), 0:10, :]
    window[26:28, :] += received[lax.rem(j + 3, peers), 0:2, :]
    window[0:2, :] += received[lax.rem(j - 3 + peers, peers), 8:10, :]
    sums = sum_over_row(place, received, 8, 2)
    tile_out[...] = jnp.zeros(tile_out.shape, F32)
    edges = pick_edges(window[...])
    tile_out[0:4, 0:32] = edges[0:4]
    tile_out[4:6, :] = sums[2:4]
    copies_of(tile_out, sent)


def last_kernel(place, received, loaded, pressure, window, tile_out):
    j = place[0]
    peers = received.shape[0]
    window[...] = pressure[...]
    window[2:26, :] += loaded[...]
    window[10:20, :] += received[lax.rem(j + 1, peers), 0:10, :]
    window[8:18, :] += received[lax.rem(j - 1 + peers, peers), 0:10, :]
    window[18:20, :] += received[lax.rem(j + 2, peers), 0:2, :]
    window[8:10, :] += received[lax.rem(j - 2 + peers, peers), 8:10, :]
    tile_out[...] = jnp.zeros(tile_out.shape, F32)
    tile_out[0:4, 0:32] = pick_edges(window[...])[0:4]


def beside(place, left, right):
    g = place[1]
    row = iota((8, 128), 0)
    edges = jnp.where((row < 2) & (g < place[3] - 1), right, 0.0)
    edges += jnp.where((row >= 2) & (row < 4) & (g > 0), left, 0.0)
    return spread_edges(edges, 128)


def flow(place, window, window_side, mobility, mobility_side):
    j = place[0]
    p = jnp.concatenate([window, window_side], axis=1)
    lane = iota((32, 128), 1)
    m_side = jnp.where((lane == 0) | (lane == 127), mobility_side, 0.0)
    m = jnp.concatenate([mobility, m_side], axis=1)
    rows = place[4]
    row = lax.rem(iota((32, 256), 0) + (j * 8 - HALO + rows), jnp.full((32, 256), 0, jnp.int32) + rows)
    for step in range(2):
        up = jnp.where(row == 0, 0.0, pltpu.roll(p, 1, 0))
        down = jnp.where(row == rows - 1, 0.0, pltpu.roll(p, 31, 0))
        sides = pltpu.roll(p, 1, 1) + pltpu.roll(p, 255, 1)
        p = p + m * (up + down + sides - 4.0 * p)
    return p[:, 0:128]


def update(place, received, tile, near, refs, window, slip_out, loaded_out):
    (slip, prestress, basis, normal, friction, compliance, state, dilation, pick, weight, h) = refs
    g = place[1]
    row, lane = iota((8, 128), 0), iota((8, 128), 1)
    level = lane // RK + jnp.where(row == 5, 8, 0)
    bit = jnp.maximum(level - GX_BITS, 0)
    own = jnp.right_shift(jnp.zeros((8, 128), jnp.int32) + g, bit)
    total = jnp.where((level < GX_BITS) & (row == 4), tile[...], 0.0)
    within = (level >= GX_BITS) & (level < LV) & ((row == 4) | (row == 5))
    for p in range(received.shape[0]):
        theirs = jnp.right_shift(jnp.full((8, 128), p, jnp.int32), bit)
        total += jnp.where(within & (theirs == jnp.bitwise_xor(own, 1)), received[p], 0.0)
    parts = jnp.where(iota((8, RK), 0) == 4, dot(total, h[0:128, :]), 0.0)
    parts += jnp.where(iota((8, RK), 0) == 5, dot(total, h[128:256, :]), 0.0)
    incoming = dot(parts, jnp.ones((8, 128), F32), TN)

    cells = window[2:26, :]
    both = jnp.concatenate([cells, pltpu.roll(cells, 127, 1)], axis=0)
    split = thirds(both)
    found = dot(split, pick[...], NN, None)
    found = (found[0:48] + found[48:96] + found[96:144]) * weight[...]
    at_row = jnp.sum(found, axis=0, keepdims=True)

    for c in range(8):
        for i in range(3):
            far = jnp.sum(basis[c, i] * incoming, axis=0, keepdims=True)
            slip_out[i, c : c + 1, :] = far
    at_elements = jnp.concatenate([at_row[:, c * 128 : (c + 1) * 128] for c in range(8)], axis=0)
    stress = [prestress[i] - (near[i] + slip_out[i]) for i in range(3)]
    effective = normal[...] - at_elements
    magnitude = jnp.sqrt(stress[0] * stress[0] + stress[1] * stress[1] + stress[2] * stress[2] + 1.0)
    factor = jnp.maximum(1.0 - friction[...] * effective / magnitude, 0.0)
    scaled = state[...].astype(F32) * compliance[...] * factor
    steps = [scaled * stress[i] for i in range(3)]
    for i in range(3):
        slip_out[i] = slip[i] + steps[i]
    dilated = dilation[...] * (steps[0] * steps[0] + steps[1] * steps[1] + steps[2] * steps[2])
    dilated_row = jnp.concatenate([dilated[c : c + 1, :] for c in range(8)], axis=1)
    spread = dot(thirds(weight[...] * dilated_row), pick[...], NT, None)
    spread = spread[0:48] + spread[48:96] + spread[96:144]
    loaded_out[...] = spread[0:24] + pltpu.roll(spread[24:48], 1, 1)


def send_sources(place, loaded, ahead, behind, sent):
    j = place[0]
    peers = sent.shape[0]
    ahead[0:10, :] = loaded[0:10, :]
    behind[0:10, :] = loaded[14:24, :]
    for p in range(peers):
        back = lax.rem(j - p + peers, peers) < peers // 2
        sent[p] = jnp.where(back, ahead[...], behind[...])


def first_update_kernel(place, received, tile, near, *refs):
    refs, (window, lifts), outs = refs[:11], refs[11:13], refs[13:]
    slip_out, loaded, down_out, up_out, sent, ahead, behind = outs
    update(place, received, tile, near, refs, window, slip_out, loaded)
    low, high = project(refs[2], lambda i, c: slip_out[i, c : c + 1, :], lifts)
    for out in (ahead, behind):
        out[...] = jnp.zeros(out.shape, F32)
        out[10:11, :] = low[0:1]
        out[11:12, :] = high[0:1]
    send_sources(place, loaded, ahead, behind, sent)
    for out, at in ((down_out, 0), (up_out, 6)):
        out[0:3] = slip_out[...]
        out[3] = loaded[at : at + 8, :]
        out[4] = loaded[at + 8 : at + 16, :]
        out[5] = jnp.zeros((8, 128), F32)
        out[5, 0:2, :] = loaded[at + 16 : at + 18, :]


def second_update_kernel(place, received, tile, near, *refs):
    refs, (window, mobility, mobility_side), outs = refs[:11], refs[11:14], refs[14:]
    slip_out, loaded, window_out, sent, ahead, behind = outs
    g = place[1]
    left = received[jnp.maximum(g - 1, 0)]
    right = received[jnp.minimum(g + 1, received.shape[0] - 1)]
    side = beside(place, left, right)
    window_out[...] = flow(place, window[...], side, mobility[...], mobility_side[...])
    update(place, received, tile, near, refs, window_out, slip_out, loaded)
    for out in (ahead, behind):
        out[...] = jnp.zeros(out.shape, F32)
    send_sources(place, loaded, ahead, behind, sent)


def side_kernel(place, received, side_out):
    g = place[1]
    left = received[jnp.maximum(g - 1, 0)]
    right = received[jnp.minimum(g + 1, received.shape[0] - 1)]
    side_out[...] = beside(place, left, right)


def final_kernel(place, window, left, right, mobility, mobility_side, out):
    side = beside(place, left[...], right[...])
    done = flow(place, window[...], side, mobility[...], mobility_side[...])
    out[...] = done[HALO : HALO + 8, :]


def shift(x, axis, steps):
    n = lax.axis_size(axis)
    return lax.ppermute(x, axis, [(i, (i + steps) % n) for i in range(n)])


def shards(
    slip_field,
    positions,
    neighbours,
    near_counts,
    cluster_basis,
    transfer,
    coupling,
    prestress,
    normal_stress,
    friction,
    compliance,
    slip_state,
    cell_index,
    cell_weight,
    dilation,
    pressure,
    mobility,
):
    nx, ny = lax.axis_size("gx"), lax.axis_size("gy")
    j, g = lax.axis_index("gx"), lax.axis_index("gy")
    rows = 8 * nx
    place = jnp.stack([j, g, g * nx + j, jnp.int32(ny), jnp.int32(rows)]).astype(jnp.int32)
    slip = slip_field.transpose(1, 0, 2)
    points = positions.transpose(1, 0, 2)
    strained = prestress.transpose(1, 0, 2)
    basis = cluster_basis.transpose(0, 2, 1, 3)
    lift_table = transfer.transpose(1, 2, 0).reshape(RK * RK, -1)
    cross_table = coupling.transpose(1, 2, 0).reshape(RK * RK, -1)
    lift_end = jnp.pad(lift_table[:, 896:], ((0, 0), (0, 1024 - lift_table.shape[1])))
    cross_end = jnp.pad(cross_table[:, 896:], ((0, 0), (0, 1024 - cross_table.shape[1])))
    slots = (neighbours - j * 8 + 8 + rows) % rows
    first_cell = cell_index[:, 0, :]
    cell_row = (first_cell // 128 - j * 8 + 8 + rows) % rows
    cell_col = first_cell % 128
    weights = cell_weight.transpose(1, 0, 2)

    g_mat, h_mat, sent = call(
        setup_kernel,
        [((256, RK), F32), ((256, RK), F32), ((nx, 8, 128), F32)],
        [place, lift_table, cross_table, lift_end, cross_end, slip, basis, pressure, mobility],
        scratch=[pltpu.VMEM((2, 3, 256, 128), F32), pltpu.SemaphoreType.DMA((6,))],
        smem=1,
        far=2,
        room=60,
    )
    both = jnp.concatenate([slip, points, pressure[None], mobility[None]], axis=0)
    both, sent = lax.optimization_barrier((both, sent))
    received = lax.all_to_all(sent, "gx", 0, 0, tiled=True)
    low = shift(both, "gx", 1)
    high = shift(both, "gx", -1)
    low_points, high_points = low[3:6], high[3:6]
    pick, weight = call(
        cells_kernel,
        [((128, 1024), BF16), ((48, 1024), F32)],
        [cell_row, cell_col, weights],
        flops=1 << 20,
    )
    mobility_side = None
    window = mobility_window = loaded = None

    for outer_step in range(2):
        (near,) = call(
            near_kernel,
            [((3, 8, 128), F32)],
            [near_counts, slots, points, low_points, high_points, slip, low, high],
            scratch=[
                pltpu.VMEM((3, 3, 8, 128), F32),
                pltpu.VMEM((3, 3, 8, 128), F32),
                pltpu.VMEM((3, 128, 128), F32),
                pltpu.VMEM((3, 128, 128), F32),
            ],
            smem=2,
            flops=1 << 28,
        )
        if outer_step == 0:
            window, mobility_window, tile, sent = call(
                first_kernel,
                [((32, 128), F32), ((32, 128), F32), ((8, 128), F32), ((ny, 8, 128), F32)],
                [place, received, low, high, pressure, mobility],
                smem=1,
            )
        else:
            window, tile, sent = call(
                between_kernel,
                [((32, 128), F32), ((8, 128), F32), ((ny, 8, 128), F32)],
                [place, received, low, high, loaded, window],
                smem=1,
            )
        early = (near, sent, pick, weight, mobility_side)
        near, sent, pick, weight, mobility_side = lax.optimization_barrier(early)
        received = lax.all_to_all(sent, "gy", 0, 0, tiled=True)
        common = [slip, strained, basis, normal_stress, friction, compliance, slip_state]
        common += [dilation, pick, weight, h_mat]
        pieces = [pltpu.VMEM((16, 128), F32), pltpu.VMEM((16, 128), F32)]
        if outer_step == 0:
            slip, loaded, down, up, sent = call(
                first_update_kernel,
                [
                    ((3, 8, 128), F32),
                    ((24, 128), F32),
                    ((6, 8, 128), F32),
                    ((6, 8, 128), F32),
                    ((nx, 16, 128), F32),
                ],
                [place, received, tile, near, *common, window, g_mat],
                scratch=pieces,
                smem=1,
            )
            (mobility_side,) = call(side_kernel, [((32, 128), F32)], [place, received], smem=1)
            received = lax.all_to_all(sent, "gx", 0, 0, tiled=True)
            low = shift(up, "gx", 1)
            high = shift(down, "gx", -1)
        else:
            slip, loaded, window, sent = call(
                second_update_kernel,
                [((3, 8, 128), F32), ((24, 128), F32), ((32, 128), F32), ((nx, 16, 128), F32)],
                [place, received, tile, near, *common, window, mobility_window, mobility_side],
                scratch=pieces,
                smem=1,
            )
            received = lax.all_to_all(sent, "gx", 0, 0, tiled=True)
    window, tile = call(
        last_kernel,
        [((32, 128), F32), ((8, 128), F32)],
        [place, received, loaded, window],
        smem=1,
    )
    left = shift(tile, "gy", 1)
    right = shift(tile, "gy", -1)
    (final_pressure,) = call(
        final_kernel,
        [((8, 128), F32)],
        [place, window, left, right, mobility_window, mobility_side],
        smem=1,
    )
    return (slip.transpose(1, 0, 2), final_pressure)


def solution(mesh):
    split = ("gy", "gx")
    in_specs = (
        P(split, None, None),
        P(split, None, None),
        P(split, None),
        P(split),
        P(split, None, None, None),
        P(),
        P(),
        P(split, None, None),
        P(split, None),
        P(split, None),
        P(split, None),
        P(split, None),
        P(split, None, None),
        P(split, None, None),
        P(split, None),
        P("gx", "gy"),
        P("gx", "gy"),
    )
    out_specs = (P(split, None, None), P("gx", "gy"))
    return jax.shard_map(shards, mesh=mesh, in_specs=in_specs, out_specs=out_specs, check_vma=False)
```

```python
import jax
import jax.numpy as jnp
from jax import lax
from jax.experimental import pallas as pl
from jax.experimental.pallas import tpu as pltpu
from jax.sharding import PartitionSpec as P

HI = lax.Precision.HIGHEST
F32 = jnp.float32
BF16 = jnp.bfloat16
SCALE = 0.04
SOFT = 0.25
LV = 9
RK = 16
GX_BITS = 5
HALO = 10

NN = (((1,), (0,)), ((), ()))
NT = (((1,), (1,)), ((), ()))
TN = (((0,), (0,)), ((), ()))


def dot(a, b, dims=NN, precision=HI):
    return lax.dot_general(a, b, dims, precision=precision, preferred_element_type=F32)


def iota(shape, dim):
    return lax.broadcasted_iota(jnp.int32, shape, dim)


def thirds(x):
    hi = x.astype(BF16)
    rest = x - hi.astype(F32)
    mid = rest.astype(BF16)
    low = (rest - mid.astype(F32)).astype(BF16)
    return jnp.concatenate([hi, mid, low], axis=0)


def split_lanes(x):
    hi = x.astype(BF16)
    rest = x - hi.astype(F32)
    mid = rest.astype(BF16)
    low = (rest - mid.astype(F32)).astype(BF16)
    return jnp.concatenate([hi, mid, low], axis=1)


def call(kernel, outs, args, scratch=(), smem=0, far=0, ends=(), flops=0, room=32):
    specs = [pl.BlockSpec(memory_space=pltpu.SMEM)] * smem
    specs += [pl.BlockSpec(memory_space=pl.ANY)] * far
    specs += [pl.BlockSpec(memory_space=pltpu.VMEM)] * (len(args) - smem - far)
    for at in ends:
        specs[at] = pl.BlockSpec((args[at].shape[0], 128), lambda i: (0, 7))
    return pl.pallas_call(
        kernel,
        out_shape=[jax.ShapeDtypeStruct(s, d) for s, d in outs],
        grid=(1,) if ends else (),
        in_specs=specs,
        out_specs=[pl.BlockSpec(memory_space=pltpu.VMEM)] * len(outs),
        scratch_shapes=list(scratch),
        compiler_params=pltpu.CompilerParams(vmem_limit_bytes=room * 1024 * 1024),
        cost_estimate=pl.CostEstimate(flops=flops, bytes_accessed=1 << 20, transcendentals=0),
    )(*args)


def setup_kernel(
    transfer,
    coupling,
    transfer_end,
    coupling_end,
    slip,
    basis,
    g_out,
    h_out,
    sent,
    held,
    sems,
):
    flat = lax.axis_index("gy") * lax.axis_size("gx") + lax.axis_index("gx")
    blocks = [pl.multiple_of(flat // 128 * 128, 128), pl.multiple_of(512 + flat // 256 * 128, 128)]
    blocks += [768, 896]
    copies = []
    for t, table in enumerate((transfer, coupling)):
        for b, start in enumerate(blocks[:3]):
            copies.append(
                pltpu.make_async_copy(
                    table.at[:, pl.ds(start, 128)], held.at[t, b], sems.at[t * 3 + b]
                )
            )
            copies[-1].start()
    total = jnp.zeros((RK, 128), F32)
    for c in range(8):
        for i in range(3):
            total += basis[c, i] * slip[i, c : c + 1, :]
    moment = dot(jnp.ones((8, 128), F32), total, NT)

    shape = (128, 256)
    level = iota(shape, 1) // RK
    first = 1024 - jnp.right_shift(jnp.full(shape, 1024, jnp.int32), level)
    wanted = first + jnp.right_shift(jnp.zeros(shape, jnp.int32) + flat, level)
    far_half = 1016 + 2 * jnp.bitwise_xor(flat // 256, 1) - LV
    wanted = jnp.where(level < LV, wanted, far_half + level)
    picks = []
    for b, start in enumerate(blocks):
        used = (level == b) if b < 3 else (level >= 3) & (level < LV + 2)
        pick = jnp.where((iota(shape, 0) + start == wanted) & used, 1.0, 0.0).astype(BF16)
        picks += [pick, pick, pick]
    picks = jnp.concatenate(picks, axis=0)
    mine = (iota((256, 256), 1) % RK) == (iota((256, 256), 0) // RK)
    inside = iota((256, 128), 1) < transfer.shape[1] - 896
    for copy in copies:
        copy.wait()

    def path_matrices(t, end):
        parts = [split_lanes(held[t, b]) for b in range(3)]
        parts.append(split_lanes(jnp.where(inside, end[...], 0.0)))
        spread = dot(jnp.concatenate(parts, axis=1), picks, NN, None)
        return jnp.sum(jnp.where(mine, spread, 0.0).reshape(RK, RK, 256), axis=0)

    lifts = path_matrices(0, transfer_end)
    across = path_matrices(1, coupling_end)
    chain = [lifts[:, l * RK : (l + 1) * RK] for l in range(LV - 1)]
    for apart in (1, 2, 4):
        chain = [
            chain[l] if l < apart else dot(chain[l], chain[l - apart]) for l in range(LV - 1)
        ]
    eye = jnp.where(iota((RK, RK), 0) == iota((RK, RK), 1), 1.0, 0.0).astype(F32)
    chain = [eye] + chain
    g_out[...] = jnp.zeros(g_out.shape, F32)
    h_out[...] = jnp.zeros(h_out.shape, F32)
    for l in range(LV):
        g_out[l * RK : (l + 1) * RK, :] = chain[l]
        h_out[l * RK : (l + 1) * RK, :] = dot(across[:, l * RK : (l + 1) * RK], chain[l])
    top = h_out[8 * RK : 9 * RK, :]
    for side in range(2):
        at = 256 + 128 * side + 7 * RK
        lane = (LV + side) * RK
        h_out[at : at + RK, :] = dot(lifts[:, lane : lane + RK], top, TN)
    low = dot(moment, g_out[0:128, :], NT)
    for p in range(sent.shape[0] // 8):
        sent[8 * p : 8 * p + 8, :] = low


def project(basis_ref, slip_rows, g_ref):
    total = jnp.zeros((RK, 128), F32)
    for c in range(8):
        for i in range(3):
            total += basis_ref[c, i] * slip_rows(i, c)
    moment = dot(jnp.ones((8, 128), F32), total, NT)
    return dot(moment, g_ref[0:128, :], NT), dot(moment, g_ref[128:256, :], NT)


def cells_kernel(row_in, col_in, weight, pick_out, weight_out):
    for c in range(8):
        lanes = slice(c * 128, (c + 1) * 128)
        row = row_in[c : c + 1, :]
        col = col_in[c : c + 1, :]
        pick_out[:, lanes] = jnp.where(iota((128, 128), 0) == col, 1.0, 0.0).astype(BF16)
        at = iota((24, 128), 0)
        for side in range(2):
            weight_out[side * 24 : side * 24 + 24, lanes] = jnp.where(
                at == row, weight[2 * side, c : c + 1, :], 0.0
            ) + jnp.where(at == row + 1, weight[2 * side + 1, c : c + 1, :], 0.0)


def near_kernel(
    counts,
    slots,
    own_points,
    low_points,
    high_points,
    own,
    low,
    high,
    near_out,
    points,
    slips,
    target,
    total,
):
    ones = jnp.ones((384, 128), BF16)
    diagonal = iota((128, 128), 0) == iota((128, 128), 1)
    for b, (p, s) in enumerate(((low_points, low), (own_points, own), (high_points, high))):
        for i in range(3):
            points[b, i] = p[i]
            slips[b, i] = s[i]
    for c in range(8):
        for i in range(3):
            wide = jnp.where(diagonal, own_points[i, c : c + 1, :], 0.0)
            target[c, i] = dot(split_lanes(wide), ones, NN, None)
    total[...] = jnp.zeros(total.shape, F32)

    def one_target(c, _):
        def one_source(k, _):
            slot = slots[c, k]
            block = slot // 8
            row = pl.ds(slot % 8, 1)
            y = [points[block, i, row, :] for i in range(3)]
            s = [slips[block, i, row, :] for i in range(3)]
            for part in range(8):
                rows = slice(part * 16, part * 16 + 16)
                r = [target[c, i, rows, :] - y[i] for i in range(3)]
                inverse = lax.rsqrt(r[0] * r[0] + r[1] * r[1] + r[2] * r[2] + SOFT)
                along = (r[0] * s[0] + r[1] * s[1] + r[2] * s[2]) * (inverse * inverse)
                for i in range(3):
                    total[c, i, rows, :] += inverse * (s[i] + along * r[i])
            return 0

        return lax.fori_loop(0, counts[c], one_source, 0)

    lax.fori_loop(0, 8, one_target, 0)
    for c in range(8):
        for i in range(3):
            summed = dot(split_lanes(total[c, i]), ones, NN, None)
            near_out[i, c : c + 1, :] = SCALE * jnp.sum(
                jnp.where(diagonal, summed, 0.0), axis=0, keepdims=True
            )


def pick_edges(window):
    row, lane = iota((8, 128), 0), iota((8, 128), 1)
    wanted = jnp.where(row < 2, row, row + 124)
    pick = jnp.where((lane == wanted) & (row < 4), 1.0, 0.0).astype(F32)
    return dot(pick, window, NT)


def sum_over_row(received, at, first):
    j = lax.axis_index("gx")
    row, lane = iota((8, 128), 0), iota((8, 128), 1)
    level = lane // RK + jnp.where(row == first + 1, 8, 0)
    own = jnp.right_shift(jnp.zeros((8, 128), jnp.int32) + j, level)
    total = jnp.zeros((8, 128), F32)
    for p in range(received.shape[0]):
        theirs = jnp.right_shift(jnp.full((8, 128), p, jnp.int32), level)
        used = (level >= GX_BITS) | (theirs == jnp.bitwise_xor(own, 1))
        total += jnp.where(used, received[p, at : at + 8, :], 0.0)
    return total


def copies_of(tile, sent):
    for p in range(sent.shape[0]):
        sent[p] = tile[...]


def between_kernel(
    received,
    low,
    high,
    first_low,
    first_high,
    loaded,
    pressure,
    mobility,
    window,
    mobility_out,
    tile_out,
    sent,
):
    j = lax.axis_index("gx")
    peers = received.shape[0]
    before = lax.rem(j - 2 + peers, peers)
    after = lax.rem(j + 2, peers)
    for out, own, at in ((window, pressure, 6), (mobility_out, mobility, 7)):
        out[...] = jnp.zeros(out.shape, F32)
        out[2:10, :] = first_low[at]
        out[10:18, :] = own[...]
        out[18:26, :] = first_high[at]
    mobility_out[1:2, :] = received[before, 12:13, :]
    mobility_out[26:27, :] = received[after, 12:13, :]
    window[2:26, :] += loaded[...]
    for i, at, size in ((3, 0, 8), (4, 8, 8), (5, 16, 2)):
        window[at : at + size, :] += low[i, 0:size, :]
        window[at + 10 : at + 10 + size, :] += high[i, 0:size, :]
    window[18:28, :] += received[after, 0:10, :]
    window[0:10, :] += received[before, 0:10, :]
    window[26:28, :] += received[lax.rem(j + 3, peers), 0:2, :]
    window[0:2, :] += received[lax.rem(j - 3 + peers, peers), 8:10, :]
    sums = sum_over_row(received, 8, 2)
    tile_out[...] = jnp.zeros(tile_out.shape, F32)
    edges = pick_edges(window[...])
    tile_out[0:4, 0:32] = edges[0:4]
    tile_out[4:6, :] = sums[2:4]
    edges = pick_edges(mobility_out[...])
    tile_out[6:7, 0:32] = edges[0:1]
    tile_out[7:8, 0:32] = edges[3:4]
    copies_of(tile_out, sent)


def last_kernel(received, loaded, pressure, window, tile_out):
    j = lax.axis_index("gx")
    peers = received.shape[0]
    window[...] = pressure[...]
    window[2:26, :] += loaded[...]
    window[10:20, :] += received[lax.rem(j + 1, peers), 0:10, :]
    window[8:18, :] += received[lax.rem(j - 1 + peers, peers), 0:10, :]
    window[18:20, :] += received[lax.rem(j + 2, peers), 0:2, :]
    window[8:10, :] += received[lax.rem(j - 2 + peers, peers), 8:10, :]
    tile_out[...] = jnp.zeros(tile_out.shape, F32)
    tile_out[0:4, 0:32] = pick_edges(window[...])[0:4]


def beside(left, right):
    g = lax.axis_index("gy")
    row, lane = iota((8, 128), 0), iota((8, 128), 1)
    from_right = (row < 2) | (row == 6)
    inside = (from_right & (g < lax.axis_size("gy") - 1)) | (~from_right & (g > 0))
    edges = jnp.where(inside, jnp.where(from_right, right, left), 0.0)[:, 0:32]
    wanted = jnp.where(row < 2, row, row + 124)
    pick = jnp.where((lane == wanted) & (row < 4), 1.0, 0.0).astype(F32)
    wanted = jnp.where(row == 6, 0, 127)
    pick_mobility = jnp.where((lane == wanted) & (row > 5), 1.0, 0.0).astype(F32)
    return dot(edges, pick, TN), dot(edges, pick_mobility, TN)


def flow(window, window_side, mobility, mobility_side):
    j = lax.axis_index("gx")
    p = jnp.concatenate([window, window_side], axis=1)
    m = jnp.concatenate([mobility, mobility_side], axis=1)
    rows = 8 * lax.axis_size("gx")
    row = lax.rem(iota((32, 256), 0) + (j * 8 - HALO + rows), jnp.full((32, 256), 0, jnp.int32) + rows)
    for step in range(2):
        up = jnp.where(row == 0, 0.0, pltpu.roll(p, 1, 0))
        down = jnp.where(row == rows - 1, 0.0, pltpu.roll(p, 31, 0))
        sides = pltpu.roll(p, 1, 1) + pltpu.roll(p, 255, 1)
        p = p + m * (up + down + sides - 4.0 * p)
    return p[:, 0:128]


def incoming_of_row(received, tile, h):
    g = lax.axis_index("gy")
    row, lane = iota((8, 128), 0), iota((8, 128), 1)
    level = lane // RK + jnp.where(row == 5, 8, 0)
    bit = jnp.maximum(level - GX_BITS, 0)
    own = jnp.right_shift(jnp.zeros((8, 128), jnp.int32) + g, bit)
    total = jnp.where((level < GX_BITS) & (row == 4), tile[...], 0.0)
    within = (level >= GX_BITS) & (level < LV) & ((row == 4) | (row == 5))
    for p in range(received.shape[0]):
        theirs = jnp.right_shift(jnp.full((8, 128), p, jnp.int32), bit)
        total += jnp.where(within & (theirs == jnp.bitwise_xor(own, 1)), received[p], 0.0)
    parts = jnp.where(iota((8, RK), 0) == 4, dot(total, h[0:128, :]), 0.0)
    return parts + jnp.where(iota((8, RK), 0) == 5, dot(total, h[128:256, :]), 0.0)


def incoming_of_all(received, h):
    ny = lax.axis_size("gy")
    flat = lax.axis_index("gy") * lax.axis_size("gx") + lax.axis_index("gx")
    row, level = iota((8, 128), 0), iota((8, 128), 1) // RK
    sibling = jnp.bitwise_xor(jnp.right_shift(jnp.zeros((8, 128), jnp.int32) + flat, level), 1)
    half = jnp.bitwise_xor(flat // 256, 1)
    sums = [jnp.zeros((8, 128), F32) for _ in range(3)]
    for at in range(0, received.shape[0], 8):
        theirs = received[at : at + 8, :]
        node = (at % ny + row) * lax.axis_size("gx") + at // ny
        upper = jnp.right_shift(node, 7)
        sums[0] += jnp.where(jnp.right_shift(node, level) == sibling, theirs, 0.0)
        sums[1] += jnp.where(upper == 2 * half, theirs, 0.0)
        sums[2] += jnp.where(upper == 2 * half + 1, theirs, 0.0)
    parts = dot(sums[0], h[0:128, :]) + dot(sums[1], h[256:384, :])
    return parts + dot(sums[2], h[384:512, :])


def update(parts, cells, near, refs, slip_out, loaded_out):
    (slip, prestress, basis, normal, friction, compliance, state, dilation, pick, weight) = refs
    incoming = dot(parts, jnp.ones((8, 128), F32), TN)

    both = jnp.concatenate([cells, pltpu.roll(cells, 127, 1)], axis=0)
    split = thirds(both)
    found = dot(split, pick[...], NN, None)
    found = (found[0:48] + found[48:96] + found[96:144]) * weight[...]
    at_row = jnp.sum(found, axis=0, keepdims=True)

    for c in range(8):
        for i in range(3):
            far = jnp.sum(basis[c, i] * incoming, axis=0, keepdims=True)
            slip_out[i, c : c + 1, :] = far
    at_elements = jnp.concatenate([at_row[:, c * 128 : (c + 1) * 128] for c in range(8)], axis=0)
    stress = [prestress[i] - (near[i] + slip_out[i]) for i in range(3)]
    effective = normal[...] - at_elements
    magnitude = jnp.sqrt(stress[0] * stress[0] + stress[1] * stress[1] + stress[2] * stress[2] + 1.0)
    factor = jnp.maximum(1.0 - friction[...] * effective / magnitude, 0.0)
    scaled = state[...].astype(F32) * compliance[...] * factor
    steps = [scaled * stress[i] for i in range(3)]
    for i in range(3):
        slip_out[i] = slip[i] + steps[i]
    dilated = dilation[...] * (steps[0] * steps[0] + steps[1] * steps[1] + steps[2] * steps[2])
    dilated_row = jnp.concatenate([dilated[c : c + 1, :] for c in range(8)], axis=1)
    spread = dot(thirds(weight[...] * dilated_row), pick[...], NT, None)
    spread = spread[0:48] + spread[48:96] + spread[96:144]
    loaded_out[...] = spread[0:24] + pltpu.roll(spread[24:48], 1, 1)


def send_sources(ahead, behind, sent):
    j = lax.axis_index("gx")
    peers = sent.shape[0]
    for p in range(peers):
        back = lax.rem(j - p + peers, peers) < peers // 2
        sent[p] = jnp.where(back, ahead[...], behind[...])


def first_update_kernel(received, low, high, pressure, mobility, lifts, h, near, *refs):
    refs, outs = refs[:10], refs[10:]
    slip_out, loaded, down_out, up_out, sent, ahead, behind = outs
    cells = jnp.concatenate([low[6], pressure[...], high[6]], axis=0)
    update(incoming_of_all(received, h), cells, near, refs, slip_out, loaded)
    low_row, high_row = project(refs[2], lambda i, c: slip_out[i, c : c + 1, :], lifts)
    ahead[...] = jnp.zeros(ahead.shape, F32)
    behind[...] = jnp.zeros(behind.shape, F32)
    ahead[0:10, :] = loaded[0:10, :]
    behind[0:10, :] = loaded[14:24, :]
    ahead[8:10, :] += pressure[0:2, :]
    behind[0:2, :] += pressure[6:8, :]
    ahead[12:13, :] = mobility[0:1, :]
    behind[12:13, :] = mobility[7:8, :]
    for out in (ahead, behind):
        out[10:11, :] = low_row[0:1]
        out[11:12, :] = high_row[0:1]
    send_sources(ahead, behind, sent)
    for out, at in ((down_out, 0), (up_out, 6)):
        out[0:3] = slip_out[...]
        out[3] = loaded[at : at + 8, :]
        out[4] = loaded[at + 8 : at + 16, :]
        out[5] = jnp.zeros((8, 128), F32)
        out[5, 0:2, :] = loaded[at + 16 : at + 18, :]


def second_update_kernel(received, tile, window, mobility, h, near, *refs):
    refs, outs = refs[:10], refs[10:]
    slip_out, loaded, window_out, side_out, sent, ahead, behind = outs
    g = lax.axis_index("gy")
    left = received[jnp.maximum(g - 1, 0)]
    right = received[jnp.minimum(g + 1, received.shape[0] - 1)]
    side, mobility_side = beside(left, right)
    side_out[...] = mobility_side
    window_out[...] = flow(window[...], side, mobility[...], mobility_side)
    parts = incoming_of_row(received, tile, h)
    update(parts, window_out[2:26, :], near, refs, slip_out, loaded)
    ahead[...] = jnp.zeros(ahead.shape, F32)
    behind[...] = jnp.zeros(behind.shape, F32)
    ahead[0:10, :] = loaded[0:10, :]
    behind[0:10, :] = loaded[14:24, :]
    send_sources(ahead, behind, sent)


def final_kernel(window, left, right, mobility, mobility_side, out):
    side, _ = beside(left[...], right[...])
    done = flow(window[...], side, mobility[...], mobility_side[...])
    out[...] = done[HALO : HALO + 8, :]


def shift(x, axis, steps):
    n = lax.axis_size(axis)
    return lax.ppermute(x, axis, [(i, (i + steps) % n) for i in range(n)])


def shards(
    slip_field,
    positions,
    neighbours,
    near_counts,
    cluster_basis,
    transfer,
    coupling,
    prestress,
    normal_stress,
    friction,
    compliance,
    slip_state,
    cell_index,
    cell_weight,
    dilation,
    pressure,
    mobility,
):
    nx, ny = lax.axis_size("gx"), lax.axis_size("gy")
    j, g = lax.axis_index("gx"), lax.axis_index("gy")
    rows = 8 * nx
    slip = slip_field.transpose(1, 0, 2)
    points = positions.transpose(1, 0, 2)
    strained = prestress.transpose(1, 0, 2)
    basis = cluster_basis.transpose(0, 2, 1, 3)
    lift_table = transfer.transpose(1, 2, 0).reshape(RK * RK, -1)
    cross_table = coupling.transpose(1, 2, 0).reshape(RK * RK, -1)
    slots = (neighbours - j * 8 + 8 + rows) % rows

    g_mat, h_mat, sent = call(
        setup_kernel,
        [((256, RK), F32), ((512, RK), F32), ((nx * ny, 128), F32)],
        [lift_table, cross_table, lift_table, cross_table, slip, basis],
        scratch=[pltpu.VMEM((2, 3, 256, 128), F32), pltpu.SemaphoreType.DMA((6,))],
        far=2,
        ends=(2, 3),
        room=60,
    )
    both = jnp.concatenate([slip, points, pressure[None], mobility[None]], axis=0)
    sent, cell_index, cell_weight = lax.optimization_barrier((sent, cell_index, cell_weight))
    first_cell = cell_index[:, 0, :]
    cell_row = (first_cell // 128 - j * 8 + 8 + rows) % rows
    cell_col = first_cell % 128
    weights = cell_weight.transpose(1, 0, 2)
    received = lax.all_to_all(
        sent.reshape(nx * ny, 1, 128), ("gx", "gy"), 0, 0, tiled=True
    ).reshape(nx * ny, 128)
    pick, weight = call(
        cells_kernel,
        [((128, 1024), BF16), ((48, 1024), F32)],
        [cell_row, cell_col, weights],
        flops=1 << 28,
    )
    both, pick = lax.optimization_barrier((both, pick))
    first_low = shift(both, "gx", 1)
    first_high = shift(both, "gx", -1)
    low_points, high_points = first_low[3:6], first_high[3:6]

    def near_field(slip, low, high):
        return call(
            near_kernel,
            [((3, 8, 128), F32)],
            [near_counts, slots, points, low_points, high_points, slip, low, high],
            scratch=[
                pltpu.VMEM((3, 3, 8, 128), F32),
                pltpu.VMEM((3, 3, 8, 128), F32),
                pltpu.VMEM((8, 3, 128, 128), F32),
                pltpu.VMEM((8, 3, 128, 128), F32),
            ],
            smem=2,
            flops=1 << 28,
        )[0]

    pieces = [pltpu.VMEM((16, 128), F32), pltpu.VMEM((16, 128), F32)]
    common = [strained, basis, normal_stress, friction, compliance, slip_state, dilation]
    common += [pick, weight]
    near = near_field(slip, first_low, first_high)
    slip, loaded, down, up, sent = call(
        first_update_kernel,
        [
            ((3, 8, 128), F32),
            ((24, 128), F32),
            ((6, 8, 128), F32),
            ((6, 8, 128), F32),
            ((nx, 16, 128), F32),
        ],
        [received, first_low, first_high, pressure, mobility, g_mat, h_mat, near, slip, *common],
        scratch=pieces,
    )
    received = lax.all_to_all(sent, "gx", 0, 0, tiled=True)
    low = shift(up, "gx", 1)
    high = shift(down, "gx", -1)
    window, mobility_window, tile, sent = call(
        between_kernel,
        [((32, 128), F32), ((32, 128), F32), ((8, 128), F32), ((ny, 8, 128), F32)],
        [received, low, high, first_low, first_high, loaded, pressure, mobility],
    )
    received = lax.all_to_all(sent, "gy", 0, 0, tiled=True)
    near_slip, sent = lax.optimization_barrier((slip, sent))
    near = near_field(near_slip, low, high)
    slip, loaded, window, mobility_side, sent = call(
        second_update_kernel,
        [
            ((3, 8, 128), F32),
            ((24, 128), F32),
            ((32, 128), F32),
            ((32, 128), F32),
            ((nx, 16, 128), F32),
        ],
        [received, tile, window, mobility_window, h_mat, near, slip, *common],
        scratch=pieces,
    )
    received = lax.all_to_all(sent, "gx", 0, 0, tiled=True)
    window, tile = call(
        last_kernel,
        [((32, 128), F32), ((8, 128), F32)],
        [received, loaded, window],
    )
    left = shift(tile, "gy", 1)
    right = shift(tile, "gy", -1)
    (final_pressure,) = call(
        final_kernel,
        [((8, 128), F32)],
        [window, left, right, mobility_window, mobility_side],
    )
    return (slip.transpose(1, 0, 2), final_pressure)


def solution(mesh):
    split = ("gy", "gx")
    in_specs = (
        P(split, None, None),
        P(split, None, None),
        P(split, None),
        P(split),
        P(split, None, None, None),
        P(),
        P(),
        P(split, None, None),
        P(split, None),
        P(split, None),
        P(split, None),
        P(split, None),
        P(split, None, None),
        P(split, None, None),
        P(split, None),
        P("gx", "gy"),
        P("gx", "gy"),
    )
    out_specs = (P(split, None, None), P("gx", "gy"))
    return jax.shard_map(shards, mesh=mesh, in_specs=in_specs, out_specs=out_specs, check_vma=False)
```

```python
import functools

import jax
import jax.numpy as jnp
from jax import lax
from jax.experimental import pallas as pl
from jax.experimental.pallas import tpu as pltpu
from jax.sharding import PartitionSpec as P

HI = lax.Precision.HIGHEST
F32 = jnp.float32
BF16 = jnp.bfloat16
SCALE = 0.04
SOFT = 0.25
LV = 9
RK = 16
GX_BITS = 5
HALO = 10

NN = (((1,), (0,)), ((), ()))
NT = (((1,), (1,)), ((), ()))
TN = (((0,), (0,)), ((), ()))


def dot(a, b, dims=NN, precision=HI):
    return lax.dot_general(a, b, dims, precision=precision, preferred_element_type=F32)


def iota(shape, dim):
    return lax.broadcasted_iota(jnp.int32, shape, dim)


def thirds(x):
    hi = x.astype(BF16)
    rest = x - hi.astype(F32)
    mid = rest.astype(BF16)
    low = (rest - mid.astype(F32)).astype(BF16)
    return jnp.concatenate([hi, mid, low], axis=0)


def split_lanes(x):
    hi = x.astype(BF16)
    rest = x - hi.astype(F32)
    mid = rest.astype(BF16)
    low = (rest - mid.astype(F32)).astype(BF16)
    return jnp.concatenate([hi, mid, low], axis=1)


def call(kernel, outs, args, scratch=(), smem=0, far=0, ends=(), flops=0, room=32):
    specs = [pl.BlockSpec(memory_space=pltpu.SMEM)] * smem
    specs += [pl.BlockSpec(memory_space=pl.ANY)] * far
    specs += [pl.BlockSpec(memory_space=pltpu.VMEM)] * (len(args) - smem - far)
    for at in ends:
        specs[at] = pl.BlockSpec((args[at].shape[0], 128), lambda i: (0, 7))
    return pl.pallas_call(
        kernel,
        out_shape=[jax.ShapeDtypeStruct(s, d) for s, d in outs],
        grid=(1,) if ends else (),
        in_specs=specs,
        out_specs=[pl.BlockSpec(memory_space=pltpu.VMEM)] * len(outs),
        scratch_shapes=list(scratch),
        compiler_params=pltpu.CompilerParams(vmem_limit_bytes=room * 1024 * 1024),
        cost_estimate=pl.CostEstimate(flops=flops, bytes_accessed=1 << 20, transcendentals=0),
    )(*args)


def setup_kernel(
    transfer,
    coupling,
    transfer_end,
    coupling_end,
    slip,
    basis,
    g_out,
    h_out,
    sent,
    held,
    sems,
):
    flat = lax.axis_index("gy") * lax.axis_size("gx") + lax.axis_index("gx")
    blocks = [pl.multiple_of(flat // 128 * 128, 128), pl.multiple_of(512 + flat // 256 * 128, 128)]
    blocks += [768, 896]
    copies = []
    for t, table in enumerate((transfer, coupling)):
        for b, start in enumerate(blocks[:3]):
            copies.append(
                pltpu.make_async_copy(
                    table.at[:, pl.ds(start, 128)], held.at[t, b], sems.at[t * 3 + b]
                )
            )
            copies[-1].start()
    total = jnp.zeros((RK, 128), F32)
    for c in range(8):
        for i in range(3):
            total += basis[c, i] * slip[i, c : c + 1, :]
    moment = dot(jnp.ones((8, 128), F32), total, NT)

    shape = (128, 256)
    level = iota(shape, 1) // RK
    first = 1024 - jnp.right_shift(jnp.full(shape, 1024, jnp.int32), level)
    wanted = first + jnp.right_shift(jnp.zeros(shape, jnp.int32) + flat, level)
    far_half = 1016 + 2 * jnp.bitwise_xor(flat // 256, 1) - LV
    wanted = jnp.where(level < LV, wanted, far_half + level)
    picks = []
    for b, start in enumerate(blocks):
        used = (level == b) if b < 3 else (level >= 3) & (level < LV + 2)
        pick = jnp.where((iota(shape, 0) + start == wanted) & used, 1.0, 0.0).astype(BF16)
        picks += [pick, pick, pick]
    picks = jnp.concatenate(picks, axis=0)
    mine = (iota((256, 256), 1) % RK) == (iota((256, 256), 0) // RK)
    inside = iota((256, 128), 1) < transfer.shape[1] - 896
    for copy in copies:
        copy.wait()

    def path_matrices(t, end):
        parts = [split_lanes(held[t, b]) for b in range(3)]
        parts.append(split_lanes(jnp.where(inside, end[...], 0.0)))
        spread = dot(jnp.concatenate(parts, axis=1), picks, NN, None)
        return jnp.sum(jnp.where(mine, spread, 0.0).reshape(RK, RK, 256), axis=0)

    lifts = path_matrices(0, transfer_end)
    across = path_matrices(1, coupling_end)
    chain = [lifts[:, l * RK : (l + 1) * RK] for l in range(LV - 1)]
    for apart in (1, 2, 4):
        chain = [
            chain[l] if l < apart else dot(chain[l], chain[l - apart]) for l in range(LV - 1)
        ]
    eye = jnp.where(iota((RK, RK), 0) == iota((RK, RK), 1), 1.0, 0.0).astype(F32)
    chain = [eye] + chain
    g_out[...] = jnp.zeros(g_out.shape, F32)
    h_out[...] = jnp.zeros(h_out.shape, F32)
    for l in range(LV):
        g_out[l * RK : (l + 1) * RK, :] = chain[l]
        h_out[l * RK : (l + 1) * RK, :] = dot(across[:, l * RK : (l + 1) * RK], chain[l])
    top = h_out[8 * RK : 9 * RK, :]
    for side in range(2):
        at = 256 + 128 * side + 7 * RK
        lane = (LV + side) * RK
        h_out[at : at + RK, :] = dot(lifts[:, lane : lane + RK], top, TN)
    low = dot(moment, g_out[0:128, :], NT)
    for p in range(sent.shape[0] // 8):
        sent[8 * p : 8 * p + 8, :] = low


def project(basis_ref, slip_rows, g_ref):
    total = jnp.zeros((RK, 128), F32)
    for c in range(8):
        for i in range(3):
            total += basis_ref[c, i] * slip_rows(i, c)
    moment = dot(jnp.ones((8, 128), F32), total, NT)
    return dot(moment, g_ref[0:128, :], NT), dot(moment, g_ref[128:256, :], NT)


def cells_kernel(row_in, col_in, weight, pick_out, weight_out):
    for c in range(8):
        lanes = slice(c * 128, (c + 1) * 128)
        row = row_in[c : c + 1, :]
        col = col_in[c : c + 1, :]
        pick_out[:, lanes] = jnp.where(iota((128, 128), 0) == col, 1.0, 0.0).astype(BF16)
        at = iota((24, 128), 0)
        for side in range(2):
            weight_out[side * 24 : side * 24 + 24, lanes] = jnp.where(
                at == row, weight[2 * side, c : c + 1, :], 0.0
            ) + jnp.where(at == row + 1, weight[2 * side + 1, c : c + 1, :], 0.0)


def add_pairs(counts, slots, target, total, points, slips, wanted):
    def one_target(c, _):
        def one_source(k, _):
            slot = slots[c, k]
            block = slot // 8
            row = pl.ds(slot % 8, 1)

            def add():
                y = [points(block)[i, row, :] for i in range(3)]
                s = [slips(block)[i, row, :] for i in range(3)]
                for part in range(8):
                    rows = slice(part * 16, part * 16 + 16)
                    r = [target[c, i, rows, :] - y[i] for i in range(3)]
                    inverse = lax.rsqrt(r[0] * r[0] + r[1] * r[1] + r[2] * r[2] + SOFT)
                    along = (r[0] * s[0] + r[1] * s[1] + r[2] * s[2]) * (inverse * inverse)
                    for i in range(3):
                        total[c, i, rows, :] += inverse * (s[i] + along * r[i])

            if wanted is None:
                add()
            else:
                pl.when(wanted(block))(add)
            return 0

        return lax.fori_loop(0, counts[c], one_source, 0)

    lax.fori_loop(0, 8, one_target, 0)


def near_own_kernel(counts, slots, own_points, own, target, total):
    ones = jnp.ones((384, 128), BF16)
    diagonal = iota((128, 128), 0) == iota((128, 128), 1)
    for c in range(8):
        for i in range(3):
            wide = jnp.where(diagonal, own_points[i, c : c + 1, :], 0.0)
            target[c, i] = dot(split_lanes(wide), ones, NN, None)
    total[...] = jnp.zeros(total.shape, F32)
    add_pairs(counts, slots, target, total, lambda b: own_points, lambda b: own, lambda b: b == 1)


def near_rest_kernel(whole, counts, slots, target, partial, *refs):
    (own_points, low_points, high_points, own, low, high, near_out, points, slips, total) = refs
    for b, (p, s) in enumerate(((low_points, low), (own_points, own), (high_points, high))):
        for i in range(3):
            points[b, i] = p[i]
            slips[b, i] = s[i]
    total[...] = jnp.zeros(total.shape, F32) if whole else partial[...]
    wanted = None if whole else lambda b: b != 1
    add_pairs(counts, slots, target, total, lambda b: points.at[b], lambda b: slips.at[b], wanted)
    ones = jnp.ones((384, 128), BF16)
    diagonal = iota((128, 128), 0) == iota((128, 128), 1)
    for c in range(8):
        for i in range(3):
            summed = dot(split_lanes(total[c, i]), ones, NN, None)
            near_out[i, c : c + 1, :] = SCALE * jnp.sum(
                jnp.where(diagonal, summed, 0.0), axis=0, keepdims=True
            )


def pack_kernel(after, slip, points, pressure, mobility, out):
    out[0:3] = slip[...]
    out[3:6] = points[...]
    out[6] = pressure[...]
    out[7] = mobility[...]


def pick_edges(window):
    row, lane = iota((8, 128), 0), iota((8, 128), 1)
    wanted = jnp.where(row < 2, row, row + 124)
    pick = jnp.where((lane == wanted) & (row < 4), 1.0, 0.0).astype(F32)
    return dot(pick, window, NT)


def sum_over_row(received, at, first):
    j = lax.axis_index("gx")
    row, lane = iota((8, 128), 0), iota((8, 128), 1)
    level = lane // RK + jnp.where(row == first + 1, 8, 0)
    own = jnp.right_shift(jnp.zeros((8, 128), jnp.int32) + j, level)
    total = jnp.zeros((8, 128), F32)
    for p in range(received.shape[0]):
        theirs = jnp.right_shift(jnp.full((8, 128), p, jnp.int32), level)
        used = (level >= GX_BITS) | (theirs == jnp.bitwise_xor(own, 1))
        total += jnp.where(used, received[p, at : at + 8, :], 0.0)
    return total


def copies_of(tile, sent):
    for p in range(sent.shape[0]):
        sent[p] = tile[...]


def between_kernel(
    received,
    low,
    high,
    first_low,
    first_high,
    loaded,
    pressure,
    mobility,
    window,
    mobility_out,
    tile_out,
    sent,
):
    j = lax.axis_index("gx")
    peers = received.shape[0]
    before = lax.rem(j - 2 + peers, peers)
    after = lax.rem(j + 2, peers)
    for out, own, at in ((window, pressure, 6), (mobility_out, mobility, 7)):
        out[...] = jnp.zeros(out.shape, F32)
        out[2:10, :] = first_low[at]
        out[10:18, :] = own[...]
        out[18:26, :] = first_high[at]
    mobility_out[1:2, :] = received[before, 12:13, :]
    mobility_out[26:27, :] = received[after, 12:13, :]
    window[2:26, :] += loaded[...]
    for i, at, size in ((3, 0, 8), (4, 8, 8), (5, 16, 2)):
        window[at : at + size, :] += low[i, 0:size, :]
        window[at + 10 : at + 10 + size, :] += high[i, 0:size, :]
    window[18:28, :] += received[after, 0:10, :]
    window[0:10, :] += received[before, 0:10, :]
    window[26:28, :] += received[lax.rem(j + 3, peers), 0:2, :]
    window[0:2, :] += received[lax.rem(j - 3 + peers, peers), 8:10, :]
    sums = sum_over_row(received, 8, 2)
    tile_out[...] = jnp.zeros(tile_out.shape, F32)
    edges = pick_edges(window[...])
    tile_out[0:4, 0:32] = edges[0:4]
    tile_out[4:6, :] = sums[2:4]
    edges = pick_edges(mobility_out[...])
    tile_out[6:7, 0:32] = edges[0:1]
    tile_out[7:8, 0:32] = edges[3:4]
    copies_of(tile_out, sent)


def last_kernel(received, low, high, loaded, pressure, window, tile_out):
    j = lax.axis_index("gx")
    peers = received.shape[0]
    window[...] = pressure[...]
    window[2:26, :] += loaded[...]
    for i, size in ((0, 8), (1, 2)):
        window[8 + 8 * i : 8 + 8 * i + size, :] += low[i, 0:size, :]
        window[10 + 8 * i : 10 + 8 * i + size, :] += high[i, 0:size, :]
    window[18:20, :] += received[lax.rem(j + 2, peers), 0:2, :]
    window[8:10, :] += received[lax.rem(j - 2 + peers, peers), 0:2, :]
    tile_out[...] = jnp.zeros(tile_out.shape, F32)
    tile_out[0:4, 0:32] = pick_edges(window[...])[0:4]


def beside(left, right):
    g = lax.axis_index("gy")
    row, lane = iota((8, 128), 0), iota((8, 128), 1)
    from_right = (row < 2) | (row == 6)
    inside = (from_right & (g < lax.axis_size("gy") - 1)) | (~from_right & (g > 0))
    edges = jnp.where(inside, jnp.where(from_right, right, left), 0.0)[:, 0:32]
    wanted = jnp.where(row < 2, row, row + 124)
    pick = jnp.where((lane == wanted) & (row < 4), 1.0, 0.0).astype(F32)
    wanted = jnp.where(row == 6, 0, 127)
    pick_mobility = jnp.where((lane == wanted) & (row > 5), 1.0, 0.0).astype(F32)
    return dot(edges, pick, TN), dot(edges, pick_mobility, TN)


def flow(window, window_side, mobility, mobility_side):
    j = lax.axis_index("gx")
    p = jnp.concatenate([window, window_side], axis=1)
    m = jnp.concatenate([mobility, mobility_side], axis=1)
    rows = 8 * lax.axis_size("gx")
    row = lax.rem(iota((32, 256), 0) + (j * 8 - HALO + rows), jnp.full((32, 256), 0, jnp.int32) + rows)
    for step in range(2):
        up = jnp.where(row == 0, 0.0, pltpu.roll(p, 1, 0))
        down = jnp.where(row == rows - 1, 0.0, pltpu.roll(p, 31, 0))
        sides = pltpu.roll(p, 1, 1) + pltpu.roll(p, 255, 1)
        p = p + m * (up + down + sides - 4.0 * p)
    return p[:, 0:128]


def incoming_of_row(received, tile, h):
    g = lax.axis_index("gy")
    row, lane = iota((8, 128), 0), iota((8, 128), 1)
    level = lane // RK + jnp.where(row == 5, 8, 0)
    bit = jnp.maximum(level - GX_BITS, 0)
    own = jnp.right_shift(jnp.zeros((8, 128), jnp.int32) + g, bit)
    total = jnp.where((level < GX_BITS) & (row == 4), tile[...], 0.0)
    within = (level >= GX_BITS) & (level < LV) & ((row == 4) | (row == 5))
    for p in range(received.shape[0]):
        theirs = jnp.right_shift(jnp.full((8, 128), p, jnp.int32), bit)
        total += jnp.where(within & (theirs == jnp.bitwise_xor(own, 1)), received[p], 0.0)
    parts = jnp.where(iota((8, RK), 0) == 4, dot(total, h[0:128, :]), 0.0)
    return parts + jnp.where(iota((8, RK), 0) == 5, dot(total, h[128:256, :]), 0.0)


def incoming_of_all(received, h):
    ny = lax.axis_size("gy")
    flat = lax.axis_index("gy") * lax.axis_size("gx") + lax.axis_index("gx")
    row, level = iota((8, 128), 0), iota((8, 128), 1) // RK
    sibling = jnp.bitwise_xor(jnp.right_shift(jnp.zeros((8, 128), jnp.int32) + flat, level), 1)
    half = jnp.bitwise_xor(flat // 256, 1)
    sums = [jnp.zeros((8, 128), F32) for _ in range(3)]
    for at in range(0, received.shape[0], 8):
        theirs = received[at : at + 8, :]
        node = (at % ny + row) * lax.axis_size("gx") + at // ny
        upper = jnp.right_shift(node, 7)
        sums[0] += jnp.where(jnp.right_shift(node, level) == sibling, theirs, 0.0)
        sums[1] += jnp.where(upper == 2 * half, theirs, 0.0)
        sums[2] += jnp.where(upper == 2 * half + 1, theirs, 0.0)
    parts = dot(sums[0], h[0:128, :]) + dot(sums[1], h[256:384, :])
    return parts + dot(sums[2], h[384:512, :])


def update(parts, cells, near, refs, slip_out, loaded_out):
    (slip, prestress, basis, normal, friction, compliance, state, dilation, pick, weight) = refs
    incoming = dot(parts, jnp.ones((8, 128), F32), TN)

    both = jnp.concatenate([cells, pltpu.roll(cells, 127, 1)], axis=0)
    split = thirds(both)
    found = dot(split, pick[...], NN, None)
    found = (found[0:48] + found[48:96] + found[96:144]) * weight[...]
    at_row = jnp.sum(found, axis=0, keepdims=True)

    for c in range(8):
        for i in range(3):
            far = jnp.sum(basis[c, i] * incoming, axis=0, keepdims=True)
            slip_out[i, c : c + 1, :] = far
    at_elements = jnp.concatenate([at_row[:, c * 128 : (c + 1) * 128] for c in range(8)], axis=0)
    stress = [prestress[i] - (near[i] + slip_out[i]) for i in range(3)]
    effective = normal[...] - at_elements
    magnitude = jnp.sqrt(stress[0] * stress[0] + stress[1] * stress[1] + stress[2] * stress[2] + 1.0)
    factor = jnp.maximum(1.0 - friction[...] * effective / magnitude, 0.0)
    scaled = state[...].astype(F32) * compliance[...] * factor
    steps = [scaled * stress[i] for i in range(3)]
    for i in range(3):
        slip_out[i] = slip[i] + steps[i]
    dilated = dilation[...] * (steps[0] * steps[0] + steps[1] * steps[1] + steps[2] * steps[2])
    dilated_row = jnp.concatenate([dilated[c : c + 1, :] for c in range(8)], axis=1)
    spread = dot(thirds(weight[...] * dilated_row), pick[...], NT, None)
    spread = spread[0:48] + spread[48:96] + spread[96:144]
    loaded_out[...] = spread[0:24] + pltpu.roll(spread[24:48], 1, 1)


def send_sources(ahead, behind, sent):
    j = lax.axis_index("gx")
    peers = sent.shape[0]
    for p in range(peers):
        back = lax.rem(j - p + peers, peers) < peers // 2
        sent[p] = jnp.where(back, ahead[...], behind[...])


def first_update_kernel(received, low, high, pressure, mobility, lifts, h, near, *refs):
    refs, outs = refs[:10], refs[10:]
    slip_out, loaded, down_out, up_out, sent, ahead, behind = outs
    cells = jnp.concatenate([low[6], pressure[...], high[6]], axis=0)
    update(incoming_of_all(received, h), cells, near, refs, slip_out, loaded)
    low_row, high_row = project(refs[2], lambda i, c: slip_out[i, c : c + 1, :], lifts)
    ahead[...] = jnp.zeros(ahead.shape, F32)
    behind[...] = jnp.zeros(behind.shape, F32)
    ahead[0:10, :] = loaded[0:10, :]
    behind[0:10, :] = loaded[14:24, :]
    ahead[8:10, :] += pressure[0:2, :]
    behind[0:2, :] += pressure[6:8, :]
    ahead[12:13, :] = mobility[0:1, :]
    behind[12:13, :] = mobility[7:8, :]
    for out in (ahead, behind):
        out[10:11, :] = low_row[0:1]
        out[11:12, :] = high_row[0:1]
    send_sources(ahead, behind, sent)
    for out, at in ((down_out, 0), (up_out, 6)):
        out[0:3] = slip_out[...]
        out[3] = loaded[at : at + 8, :]
        out[4] = loaded[at + 8 : at + 16, :]
        out[5] = jnp.zeros((8, 128), F32)
        out[5, 0:2, :] = loaded[at + 16 : at + 18, :]


def second_update_kernel(received, tile, window, mobility, h, near, *refs):
    refs, outs = refs[:10], refs[10:]
    slip_out, loaded, window_out, side_out, down_out, up_out, sent, ahead, behind = outs
    g = lax.axis_index("gy")
    left = received[jnp.maximum(g - 1, 0)]
    right = received[jnp.minimum(g + 1, received.shape[0] - 1)]
    side, mobility_side = beside(left, right)
    side_out[...] = mobility_side
    window_out[...] = flow(window[...], side, mobility[...], mobility_side)
    parts = incoming_of_row(received, tile, h)
    update(parts, window_out[2:26, :], near, refs, slip_out, loaded)
    ahead[...] = jnp.zeros(ahead.shape, F32)
    behind[...] = jnp.zeros(behind.shape, F32)
    ahead[0:2, :] = loaded[0:2, :]
    behind[0:2, :] = loaded[22:24, :]
    send_sources(ahead, behind, sent)
    for out, at in ((down_out, 0), (up_out, 14)):
        out[0] = loaded[at : at + 8, :]
        out[1] = jnp.zeros((8, 128), F32)
        out[1, 0:2, :] = loaded[at + 8 : at + 10, :]


def final_kernel(window, left, right, mobility, mobility_side, out):
    side, _ = beside(left[...], right[...])
    done = flow(window[...], side, mobility[...], mobility_side[...])
    out[...] = done[HALO : HALO + 8, :]


def shift(x, axis, steps):
    n = lax.axis_size(axis)
    return lax.ppermute(x, axis, [(i, (i + steps) % n) for i in range(n)])


def shards(
    slip_field,
    positions,
    neighbours,
    near_counts,
    cluster_basis,
    transfer,
    coupling,
    prestress,
    normal_stress,
    friction,
    compliance,
    slip_state,
    cell_index,
    cell_weight,
    dilation,
    pressure,
    mobility,
):
    nx, ny = lax.axis_size("gx"), lax.axis_size("gy")
    j, g = lax.axis_index("gx"), lax.axis_index("gy")
    rows = 8 * nx
    slip = slip_field.transpose(1, 0, 2)
    points = positions.transpose(1, 0, 2)
    strained = prestress.transpose(1, 0, 2)
    basis = cluster_basis.transpose(0, 2, 1, 3)
    lift_table = transfer.transpose(1, 2, 0).reshape(RK * RK, -1)
    cross_table = coupling.transpose(1, 2, 0).reshape(RK * RK, -1)
    slots = (neighbours - j * 8 + 8 + rows) % rows

    g_mat, h_mat, sent = call(
        setup_kernel,
        [((256, RK), F32), ((512, RK), F32), ((nx * ny, 128), F32)],
        [lift_table, cross_table, lift_table, cross_table, slip, basis],
        scratch=[pltpu.VMEM((2, 3, 256, 128), F32), pltpu.SemaphoreType.DMA((6,))],
        far=2,
        ends=(2, 3),
        room=60,
    )
    (both,) = call(
        pack_kernel,
        [((8, 8, 128), F32)],
        [h_mat, slip, points, pressure, mobility],
        far=1,
        flops=1 << 28,
    )
    sent, cell_index, cell_weight = lax.optimization_barrier((sent, cell_index, cell_weight))
    first_cell = cell_index[:, 0, :]
    cell_row = (first_cell // 128 - j * 8 + 8 + rows) % rows
    cell_col = first_cell % 128
    weights = cell_weight.transpose(1, 0, 2)
    received = lax.all_to_all(
        sent.reshape(nx * ny, 1, 128), ("gx", "gy"), 0, 0, tiled=True
    ).reshape(nx * ny, 128)
    pick, weight = call(
        cells_kernel,
        [((128, 1024), BF16), ((48, 1024), F32)],
        [cell_row, cell_col, weights],
        flops=1 << 28,
    )
    both, pick = lax.optimization_barrier((both, pick))
    first_low = shift(both, "gx", 1)
    first_high = shift(both, "gx", -1)
    low_points, high_points = first_low[3:6], first_high[3:6]

    target, partial = call(
        near_own_kernel,
        [((8, 3, 128, 128), F32), ((8, 3, 128, 128), F32)],
        [near_counts, slots, points, slip],
        smem=2,
    )

    def near_field(whole, slip, low, high):
        args = [near_counts, slots, target, target if whole else partial]
        return call(
            functools.partial(near_rest_kernel, whole),
            [((3, 8, 128), F32)],
            [*args, points, low_points, high_points, slip, low, high],
            scratch=[
                pltpu.VMEM((3, 3, 8, 128), F32),
                pltpu.VMEM((3, 3, 8, 128), F32),
                pltpu.VMEM((8, 3, 128, 128), F32),
            ],
            smem=2,
            flops=1 << 28 if whole else 0,
        )[0]

    pieces = [pltpu.VMEM((16, 128), F32), pltpu.VMEM((16, 128), F32)]
    common = [strained, basis, normal_stress, friction, compliance, slip_state, dilation]
    common += [pick, weight]
    near = near_field(False, slip, first_low, first_high)
    slip, loaded, down, up, sent = call(
        first_update_kernel,
        [
            ((3, 8, 128), F32),
            ((24, 128), F32),
            ((6, 8, 128), F32),
            ((6, 8, 128), F32),
            ((nx, 16, 128), F32),
        ],
        [received, first_low, first_high, pressure, mobility, g_mat, h_mat, near, slip, *common],
        scratch=pieces,
    )
    received = lax.all_to_all(sent, "gx", 0, 0, tiled=True)
    low = shift(up, "gx", 1)
    high = shift(down, "gx", -1)
    window, mobility_window, tile, sent = call(
        between_kernel,
        [((32, 128), F32), ((32, 128), F32), ((8, 128), F32), ((ny, 8, 128), F32)],
        [received, low, high, first_low, first_high, loaded, pressure, mobility],
    )
    received = lax.all_to_all(sent, "gy", 0, 0, tiled=True)
    near_slip, sent = lax.optimization_barrier((slip, sent))
    near = near_field(True, near_slip, low, high)
    slip, loaded, window, mobility_side, down, up, sent = call(
        second_update_kernel,
        [
            ((3, 8, 128), F32),
            ((24, 128), F32),
            ((32, 128), F32),
            ((32, 128), F32),
            ((2, 8, 128), F32),
            ((2, 8, 128), F32),
            ((nx, 8, 128), F32),
        ],
        [received, tile, window, mobility_window, h_mat, near, slip, *common],
        scratch=[pltpu.VMEM((8, 128), F32), pltpu.VMEM((8, 128), F32)],
    )
    received = lax.all_to_all(sent, "gx", 0, 0, tiled=True)
    low = shift(up, "gx", 1)
    high = shift(down, "gx", -1)
    window, tile = call(
        last_kernel,
        [((32, 128), F32), ((8, 128), F32)],
        [received, low, high, loaded, window],
    )
    left = shift(tile, "gy", 1)
    right = shift(tile, "gy", -1)
    (final_pressure,) = call(
        final_kernel,
        [((8, 128), F32)],
        [window, left, right, mobility_window, mobility_side],
    )
    return (slip.transpose(1, 0, 2), final_pressure)


def solution(mesh):
    split = ("gy", "gx")
    in_specs = (
        P(split, None, None),
        P(split, None, None),
        P(split, None),
        P(split),
        P(split, None, None, None),
        P(),
        P(),
        P(split, None, None),
        P(split, None),
        P(split, None),
        P(split, None),
        P(split, None),
        P(split, None, None),
        P(split, None, None),
        P(split, None),
        P("gx", "gy"),
        P("gx", "gy"),
    )
    out_specs = (P(split, None, None), P("gx", "gy"))
    return jax.shard_map(shards, mesh=mesh, in_specs=in_specs, out_specs=out_specs, check_vma=False)
```

```python
import functools

import jax
import jax.numpy as jnp
from jax import lax
from jax.experimental import pallas as pl
from jax.experimental.pallas import tpu as pltpu
from jax.sharding import PartitionSpec as P

HI = lax.Precision.HIGHEST
F32 = jnp.float32
BF16 = jnp.bfloat16
SCALE = 0.04
SOFT = 0.25
LV = 9
RK = 16
GX_BITS = 5
HALO = 10

NN = (((1,), (0,)), ((), ()))
NT = (((1,), (1,)), ((), ()))
TN = (((0,), (0,)), ((), ()))


def dot(a, b, dims=NN, precision=HI):
    return lax.dot_general(a, b, dims, precision=precision, preferred_element_type=F32)


def iota(shape, dim):
    return lax.broadcasted_iota(jnp.int32, shape, dim)


def thirds(x):
    hi = x.astype(BF16)
    rest = x - hi.astype(F32)
    mid = rest.astype(BF16)
    low = (rest - mid.astype(F32)).astype(BF16)
    return jnp.concatenate([hi, mid, low], axis=0)


def split_lanes(x):
    hi = x.astype(BF16)
    rest = x - hi.astype(F32)
    mid = rest.astype(BF16)
    low = (rest - mid.astype(F32)).astype(BF16)
    return jnp.concatenate([hi, mid, low], axis=1)


def call(kernel, outs, args, scratch=(), smem=0, far=0, ends=(), flops=0, room=32):
    specs = [pl.BlockSpec(memory_space=pltpu.SMEM)] * smem
    specs += [pl.BlockSpec(memory_space=pl.ANY)] * far
    specs += [pl.BlockSpec(memory_space=pltpu.VMEM)] * (len(args) - smem - far)
    for at in ends:
        specs[at] = pl.BlockSpec((args[at].shape[0], 128), lambda i: (0, 7))
    return pl.pallas_call(
        kernel,
        out_shape=[jax.ShapeDtypeStruct(s, d) for s, d in outs],
        grid=(1,) if ends else (),
        in_specs=specs,
        out_specs=[pl.BlockSpec(memory_space=pltpu.VMEM)] * len(outs),
        scratch_shapes=list(scratch),
        compiler_params=pltpu.CompilerParams(vmem_limit_bytes=room * 1024 * 1024),
        cost_estimate=pl.CostEstimate(flops=flops, bytes_accessed=1 << 20, transcendentals=0),
    )(*args)


def setup_kernel(
    transfer,
    coupling,
    transfer_end,
    coupling_end,
    slip,
    basis,
    g_out,
    h_out,
    sent,
    held,
    sems,
):
    flat = lax.axis_index("gy") * lax.axis_size("gx") + lax.axis_index("gx")
    blocks = [pl.multiple_of(flat // 128 * 128, 128), pl.multiple_of(512 + flat // 256 * 128, 128)]
    blocks += [768, 896]
    copies = []
    for t, table in enumerate((transfer, coupling)):
        for b, start in enumerate(blocks[:3]):
            copies.append(
                pltpu.make_async_copy(
                    table.at[:, pl.ds(start, 128)], held.at[t, b], sems.at[t * 3 + b]
                )
            )
            copies[-1].start()
    total = jnp.zeros((RK, 128), F32)
    for c in range(8):
        for i in range(3):
            total += basis[c, i] * slip[i, c : c + 1, :]
    moment = dot(jnp.ones((8, 128), F32), total, NT)

    shape = (128, 256)
    level = iota(shape, 1) // RK
    first = 1024 - jnp.right_shift(jnp.full(shape, 1024, jnp.int32), level)
    wanted = first + jnp.right_shift(jnp.zeros(shape, jnp.int32) + flat, level)
    far_half = 1016 + 2 * jnp.bitwise_xor(flat // 256, 1) - LV
    wanted = jnp.where(level < LV, wanted, far_half + level)
    picks = []
    for b, start in enumerate(blocks):
        used = (level == b) if b < 3 else (level >= 3) & (level < LV + 2)
        pick = jnp.where((iota(shape, 0) + start == wanted) & used, 1.0, 0.0).astype(BF16)
        picks += [pick, pick, pick]
    picks = jnp.concatenate(picks, axis=0)
    mine = (iota((256, 256), 1) % RK) == (iota((256, 256), 0) // RK)
    inside = iota((256, 128), 1) < transfer.shape[1] - 896
    for copy in copies:
        copy.wait()

    def path_matrices(t, end):
        parts = [split_lanes(held[t, b]) for b in range(3)]
        parts.append(split_lanes(jnp.where(inside, end[...], 0.0)))
        spread = dot(jnp.concatenate(parts, axis=1), picks, NN, None)
        return jnp.sum(jnp.where(mine, spread, 0.0).reshape(RK, RK, 256), axis=0)

    lifts = path_matrices(0, transfer_end)
    across = path_matrices(1, coupling_end)
    chain = [lifts[:, l * RK : (l + 1) * RK] for l in range(LV - 1)]
    for apart in (1, 2, 4):
        chain = [
            chain[l] if l < apart else dot(chain[l], chain[l - apart]) for l in range(LV - 1)
        ]
    eye = jnp.where(iota((RK, RK), 0) == iota((RK, RK), 1), 1.0, 0.0).astype(F32)
    chain = [eye] + chain
    g_out[...] = jnp.zeros(g_out.shape, F32)
    h_out[...] = jnp.zeros(h_out.shape, F32)
    for l in range(LV):
        g_out[l * RK : (l + 1) * RK, :] = chain[l]
        h_out[l * RK : (l + 1) * RK, :] = dot(across[:, l * RK : (l + 1) * RK], chain[l])
    top = h_out[8 * RK : 9 * RK, :]
    for side in range(2):
        at = 256 + 128 * side + 7 * RK
        lane = (LV + side) * RK
        h_out[at : at + RK, :] = dot(lifts[:, lane : lane + RK], top, TN)
    low = dot(moment, g_out[0:128, :], NT)
    for p in range(sent.shape[0] // 8):
        sent[8 * p : 8 * p + 8, :] = low


def project(basis_ref, slip_rows, g_ref):
    total = jnp.zeros((RK, 128), F32)
    for c in range(8):
        for i in range(3):
            total += basis_ref[c, i] * slip_rows(i, c)
    moment = dot(jnp.ones((8, 128), F32), total, NT)
    return dot(moment, g_ref[0:128, :], NT), dot(moment, g_ref[128:256, :], NT)


def cells_kernel(row_in, col_in, weight, pick_out, weight_out):
    for c in range(8):
        lanes = slice(c * 128, (c + 1) * 128)
        row = row_in[c : c + 1, :]
        col = col_in[c : c + 1, :]
        pick_out[:, lanes] = jnp.where(iota((128, 128), 0) == col, 1.0, 0.0).astype(BF16)
        at = iota((24, 128), 0)
        for side in range(2):
            weight_out[side * 24 : side * 24 + 24, lanes] = jnp.where(
                at == row, weight[2 * side, c : c + 1, :], 0.0
            ) + jnp.where(at == row + 1, weight[2 * side + 1, c : c + 1, :], 0.0)


def add_pairs(counts, slots, target, total, points, slips, wanted):
    def one_target(c, _):
        def one_source(k, _):
            slot = slots[c, k]
            block = slot // 8
            row = pl.ds(slot % 8, 1)

            def add():
                y = [points(block)[i, row, :] for i in range(3)]
                s = [slips(block)[i, row, :] for i in range(3)]
                for part in range(8):
                    rows = slice(part * 16, part * 16 + 16)
                    r = [target[c, i, rows, :] - y[i] for i in range(3)]
                    inverse = lax.rsqrt(r[0] * r[0] + r[1] * r[1] + r[2] * r[2] + SOFT)
                    along = (r[0] * s[0] + r[1] * s[1] + r[2] * s[2]) * (inverse * inverse)
                    for i in range(3):
                        total[c, i, rows, :] += inverse * (s[i] + along * r[i])

            if wanted is None:
                add()
            else:
                pl.when(wanted(block))(add)
            return 0

        return lax.fori_loop(0, counts[c], one_source, 0)

    lax.fori_loop(0, 8, one_target, 0)


def near_own_kernel(counts, slots, own_points, own, target, total):
    ones = jnp.ones((384, 128), BF16)
    diagonal = iota((128, 128), 0) == iota((128, 128), 1)
    for c in range(8):
        for i in range(3):
            wide = jnp.where(diagonal, own_points[i, c : c + 1, :], 0.0)
            target[c, i] = dot(split_lanes(wide), ones, NN, None)
    total[...] = jnp.zeros(total.shape, F32)
    add_pairs(counts, slots, target, total, lambda b: own_points, lambda b: own, lambda b: b == 1)


def near_rest_kernel(whole, counts, slots, target, partial, *refs):
    (own_points, low_points, high_points, own, low, high, near_out, points, slips, total) = refs
    for b, (p, s) in enumerate(((low_points, low), (own_points, own), (high_points, high))):
        for i in range(3):
            points[b, i] = p[i]
            slips[b, i] = s[i]
    total[...] = jnp.zeros(total.shape, F32) if whole else partial[...]
    wanted = None if whole else lambda b: b != 1
    add_pairs(counts, slots, target, total, lambda b: points.at[b], lambda b: slips.at[b], wanted)
    ones = jnp.ones((384, 128), BF16)
    diagonal = iota((128, 128), 0) == iota((128, 128), 1)
    for c in range(8):
        for i in range(3):
            summed = dot(split_lanes(total[c, i]), ones, NN, None)
            near_out[i, c : c + 1, :] = SCALE * jnp.sum(
                jnp.where(diagonal, summed, 0.0), axis=0, keepdims=True
            )


def pack_kernel(after, slip, points, pressure, mobility, out):
    out[0:3] = slip[...]
    out[3:6] = points[...]
    out[6] = pressure[...]
    out[7] = mobility[...]


def pick_edges(window):
    row, lane = iota((8, 128), 0), iota((8, 128), 1)
    wanted = jnp.where(row < 2, row, row + 124)
    pick = jnp.where((lane == wanted) & (row < 4), 1.0, 0.0).astype(F32)
    return dot(pick, window, NT)


def sum_over_row(received, at, first):
    j = lax.axis_index("gx")
    row, lane = iota((8, 128), 0), iota((8, 128), 1)
    level = lane // RK + jnp.where(row == first + 1, 8, 0)
    own = jnp.right_shift(jnp.zeros((8, 128), jnp.int32) + j, level)
    total = jnp.zeros((8, 128), F32)
    for p in range(received.shape[0]):
        theirs = jnp.right_shift(jnp.full((8, 128), p, jnp.int32), level)
        used = (level >= GX_BITS) | (theirs == jnp.bitwise_xor(own, 1))
        total += jnp.where(used, received[p, at : at + 8, :], 0.0)
    return total


def copies_of(tile, sent):
    for p in range(sent.shape[0]):
        sent[p] = tile[...]


def between_kernel(
    received,
    low,
    high,
    first_low,
    first_high,
    loaded,
    pressure,
    mobility,
    window,
    mobility_out,
    tile_out,
    sent,
):
    j = lax.axis_index("gx")
    peers = received.shape[0]
    before = lax.rem(j - 2 + peers, peers)
    after = lax.rem(j + 2, peers)
    for out, own, at in ((window, pressure, 6), (mobility_out, mobility, 7)):
        out[...] = jnp.zeros(out.shape, F32)
        out[2:10, :] = first_low[at]
        out[10:18, :] = own[...]
        out[18:26, :] = first_high[at]
    mobility_out[1:2, :] = received[before, 12:13, :]
    mobility_out[26:27, :] = received[after, 12:13, :]
    window[2:26, :] += loaded[...]
    for i, at, size in ((3, 0, 8), (4, 8, 8), (5, 16, 2)):
        window[at : at + size, :] += low[i, 0:size, :]
        window[at + 10 : at + 10 + size, :] += high[i, 0:size, :]
    window[18:28, :] += received[after, 0:10, :]
    window[0:10, :] += received[before, 0:10, :]
    window[26:28, :] += received[lax.rem(j + 3, peers), 0:2, :]
    window[0:2, :] += received[lax.rem(j - 3 + peers, peers), 8:10, :]
    sums = sum_over_row(received, 8, 2)
    tile_out[...] = jnp.zeros(tile_out.shape, F32)
    edges = pick_edges(window[...])
    tile_out[0:4, 0:32] = edges[0:4]
    tile_out[4:6, :] = sums[2:4]
    edges = pick_edges(mobility_out[...])
    tile_out[6:7, 0:32] = edges[0:1]
    tile_out[7:8, 0:32] = edges[3:4]
    copies_of(tile_out, sent)


def last_kernel(received, low, high, loaded, pressure, window, tile_out):
    j = lax.axis_index("gx")
    peers = received.shape[0]
    window[...] = pressure[...]
    window[2:26, :] += loaded[...]
    for i, size in ((0, 8), (1, 2)):
        window[8 + 8 * i : 8 + 8 * i + size, :] += low[i, 0:size, :]
        window[10 + 8 * i : 10 + 8 * i + size, :] += high[i, 0:size, :]
    window[18:20, :] += received[lax.rem(j + 2, peers), 0:2, :]
    window[8:10, :] += received[lax.rem(j - 2 + peers, peers), 0:2, :]
    tile_out[...] = jnp.zeros(tile_out.shape, F32)
    tile_out[0:4, 0:32] = pick_edges(window[...])[0:4]


def beside(left, right):
    g = lax.axis_index("gy")
    row, lane = iota((8, 128), 0), iota((8, 128), 1)
    from_right = (row < 2) | (row == 6)
    inside = (from_right & (g < lax.axis_size("gy") - 1)) | (~from_right & (g > 0))
    edges = jnp.where(inside, jnp.where(from_right, right, left), 0.0)[:, 0:32]
    wanted = jnp.where(row < 2, row, row + 124)
    pick = jnp.where((lane == wanted) & (row < 4), 1.0, 0.0).astype(F32)
    wanted = jnp.where(row == 6, 0, 127)
    pick_mobility = jnp.where((lane == wanted) & (row > 5), 1.0, 0.0).astype(F32)
    return dot(edges, pick, TN), dot(edges, pick_mobility, TN)


def flow(window, window_side, mobility, mobility_side):
    j = lax.axis_index("gx")
    p = jnp.concatenate([window, window_side], axis=1)
    m = jnp.concatenate([mobility, mobility_side], axis=1)
    rows = 8 * lax.axis_size("gx")
    row = lax.rem(iota((32, 256), 0) + (j * 8 - HALO + rows), jnp.full((32, 256), 0, jnp.int32) + rows)
    for step in range(2):
        up = jnp.where(row == 0, 0.0, pltpu.roll(p, 1, 0))
        down = jnp.where(row == rows - 1, 0.0, pltpu.roll(p, 31, 0))
        sides = pltpu.roll(p, 1, 1) + pltpu.roll(p, 255, 1)
        p = p + m * (up + down + sides - 4.0 * p)
    return p[:, 0:128]


def incoming_of_row(received, tile, h):
    g = lax.axis_index("gy")
    row, lane = iota((8, 128), 0), iota((8, 128), 1)
    level = lane // RK + jnp.where(row == 5, 8, 0)
    bit = jnp.maximum(level - GX_BITS, 0)
    own = jnp.right_shift(jnp.zeros((8, 128), jnp.int32) + g, bit)
    total = jnp.where((level < GX_BITS) & (row == 4), tile[...], 0.0)
    within = (level >= GX_BITS) & (level < LV) & ((row == 4) | (row == 5))
    for p in range(received.shape[0]):
        theirs = jnp.right_shift(jnp.full((8, 128), p, jnp.int32), bit)
        total += jnp.where(within & (theirs == jnp.bitwise_xor(own, 1)), received[p], 0.0)
    parts = jnp.where(iota((8, RK), 0) == 4, dot(total, h[0:128, :]), 0.0)
    return parts + jnp.where(iota((8, RK), 0) == 5, dot(total, h[128:256, :]), 0.0)


def incoming_of_all(received, h):
    ny = lax.axis_size("gy")
    flat = lax.axis_index("gy") * lax.axis_size("gx") + lax.axis_index("gx")
    row, level = iota((8, 128), 0), iota((8, 128), 1) // RK
    sibling = jnp.bitwise_xor(jnp.right_shift(jnp.zeros((8, 128), jnp.int32) + flat, level), 1)
    half = jnp.bitwise_xor(flat // 256, 1)
    sums = [jnp.zeros((8, 128), F32) for _ in range(3)]
    for at in range(0, received.shape[0], 8):
        theirs = received[at : at + 8, :]
        node = (at % ny + row) * lax.axis_size("gx") + at // ny
        upper = jnp.right_shift(node, 7)
        sums[0] += jnp.where(jnp.right_shift(node, level) == sibling, theirs, 0.0)
        sums[1] += jnp.where(upper == 2 * half, theirs, 0.0)
        sums[2] += jnp.where(upper == 2 * half + 1, theirs, 0.0)
    parts = dot(sums[0], h[0:128, :]) + dot(sums[1], h[256:384, :])
    return parts + dot(sums[2], h[384:512, :])


def update(parts, cells, near, refs, slip_out, loaded_out):
    (slip, prestress, basis, normal, friction, compliance, state, dilation, pick, weight) = refs
    incoming = dot(parts, jnp.ones((8, 128), F32), TN)

    both = jnp.concatenate([cells, pltpu.roll(cells, 127, 1)], axis=0)
    split = thirds(both)
    found = dot(split, pick[...], NN, None)
    found = (found[0:48] + found[48:96] + found[96:144]) * weight[...]
    at_row = jnp.sum(found, axis=0, keepdims=True)

    for c in range(8):
        for i in range(3):
            far = jnp.sum(basis[c, i] * incoming, axis=0, keepdims=True)
            slip_out[i, c : c + 1, :] = far
    at_elements = jnp.concatenate([at_row[:, c * 128 : (c + 1) * 128] for c in range(8)], axis=0)
    stress = [prestress[i] - (near[i] + slip_out[i]) for i in range(3)]
    effective = normal[...] - at_elements
    magnitude = jnp.sqrt(stress[0] * stress[0] + stress[1] * stress[1] + stress[2] * stress[2] + 1.0)
    factor = jnp.maximum(1.0 - friction[...] * effective / magnitude, 0.0)
    scaled = state[...].astype(F32) * compliance[...] * factor
    steps = [scaled * stress[i] for i in range(3)]
    for i in range(3):
        slip_out[i] = slip[i] + steps[i]
    dilated = dilation[...] * (steps[0] * steps[0] + steps[1] * steps[1] + steps[2] * steps[2])
    dilated_row = jnp.concatenate([dilated[c : c + 1, :] for c in range(8)], axis=1)
    spread = dot(thirds(weight[...] * dilated_row), pick[...], NT, None)
    spread = spread[0:48] + spread[48:96] + spread[96:144]
    loaded_out[...] = spread[0:24] + pltpu.roll(spread[24:48], 1, 1)


def send_sources(ahead, behind, sent):
    j = lax.axis_index("gx")
    peers = sent.shape[0]
    for p in range(peers):
        back = lax.rem(j - p + peers, peers) < peers // 2
        sent[p] = jnp.where(back, ahead[...], behind[...])


def first_update_kernel(received, low, high, pressure, mobility, lifts, h, near, *refs):
    refs, outs = refs[:10], refs[10:]
    slip_out, loaded, down_out, up_out, sent, ahead, behind = outs
    cells = jnp.concatenate([low[6], pressure[...], high[6]], axis=0)
    update(incoming_of_all(received, h), cells, near, refs, slip_out, loaded)
    low_row, high_row = project(refs[2], lambda i, c: slip_out[i, c : c + 1, :], lifts)
    ahead[...] = jnp.zeros(ahead.shape, F32)
    behind[...] = jnp.zeros(behind.shape, F32)
    ahead[0:10, :] = loaded[0:10, :]
    behind[0:10, :] = loaded[14:24, :]
    ahead[8:10, :] += pressure[0:2, :]
    behind[0:2, :] += pressure[6:8, :]
    ahead[12:13, :] = mobility[0:1, :]
    behind[12:13, :] = mobility[7:8, :]
    for out in (ahead, behind):
        out[10:11, :] = low_row[0:1]
        out[11:12, :] = high_row[0:1]
    send_sources(ahead, behind, sent)
    for out, at in ((down_out, 0), (up_out, 6)):
        out[0:3] = slip_out[...]
        out[3] = loaded[at : at + 8, :]
        out[4] = loaded[at + 8 : at + 16, :]
        out[5] = jnp.zeros((8, 128), F32)
        out[5, 0:2, :] = loaded[at + 16 : at + 18, :]


def second_update_kernel(received, tile, window, mobility, h, near, *refs):
    refs, outs = refs[:10], refs[10:]
    slip_out, loaded, window_out, side_out, down_out, up_out, sent, ahead, behind = outs
    g = lax.axis_index("gy")
    left = received[jnp.maximum(g - 1, 0)]
    right = received[jnp.minimum(g + 1, received.shape[0] - 1)]
    side, mobility_side = beside(left, right)
    side_out[...] = mobility_side
    window_out[...] = flow(window[...], side, mobility[...], mobility_side)
    parts = incoming_of_row(received, tile, h)
    update(parts, window_out[2:26, :], near, refs, slip_out, loaded)
    ahead[...] = jnp.zeros(ahead.shape, F32)
    behind[...] = jnp.zeros(behind.shape, F32)
    ahead[0:2, :] = loaded[0:2, :]
    behind[0:2, :] = loaded[22:24, :]
    send_sources(ahead, behind, sent)
    for out, at in ((down_out, 0), (up_out, 14)):
        out[0] = loaded[at : at + 8, :]
        out[1] = jnp.zeros((8, 128), F32)
        out[1, 0:2, :] = loaded[at + 8 : at + 10, :]


def final_kernel(window, left, right, mobility, mobility_side, out):
    side, _ = beside(left[...], right[...])
    done = flow(window[...], side, mobility[...], mobility_side[...])
    out[...] = done[HALO : HALO + 8, :]


def shift(x, axis, steps):
    n = lax.axis_size(axis)
    return lax.ppermute(x, axis, [(i, (i + steps) % n) for i in range(n)])


def with_neighbours(up, down, axis):
    n = lax.axis_size(axis)
    even = lax.axis_index(axis) % 2 == 0
    alike = up is down
    first = up if alike else jnp.where(even, up, down)
    second = up if alike else jnp.where(even, down, up)
    first = lax.ppermute(first, axis, [(i, i ^ 1) for i in range(n)])
    second = lax.ppermute(second, axis, [(i, (i + 2 * (i % 2) - 1) % n) for i in range(n)])
    return jnp.where(even, second, first), jnp.where(even, first, second)


def shards(
    slip_field,
    positions,
    neighbours,
    near_counts,
    cluster_basis,
    transfer,
    coupling,
    prestress,
    normal_stress,
    friction,
    compliance,
    slip_state,
    cell_index,
    cell_weight,
    dilation,
    pressure,
    mobility,
):
    nx, ny = lax.axis_size("gx"), lax.axis_size("gy")
    j, g = lax.axis_index("gx"), lax.axis_index("gy")
    rows = 8 * nx
    slip = slip_field.transpose(1, 0, 2)
    points = positions.transpose(1, 0, 2)
    strained = prestress.transpose(1, 0, 2)
    basis = cluster_basis.transpose(0, 2, 1, 3)
    lift_table = transfer.transpose(1, 2, 0).reshape(RK * RK, -1)
    cross_table = coupling.transpose(1, 2, 0).reshape(RK * RK, -1)
    slots = (neighbours - j * 8 + 8 + rows) % rows

    g_mat, h_mat, sent = call(
        setup_kernel,
        [((256, RK), F32), ((512, RK), F32), ((nx * ny, 128), F32)],
        [lift_table, cross_table, lift_table, cross_table, slip, basis],
        scratch=[pltpu.VMEM((2, 3, 256, 128), F32), pltpu.SemaphoreType.DMA((6,))],
        far=2,
        ends=(2, 3),
        room=60,
    )
    (both,) = call(
        pack_kernel,
        [((8, 8, 128), F32)],
        [h_mat, slip, points, pressure, mobility],
        far=1,
        flops=1 << 28,
    )
    sent, cell_index, cell_weight = lax.optimization_barrier((sent, cell_index, cell_weight))
    first_cell = cell_index[:, 0, :]
    cell_row = (first_cell // 128 - j * 8 + 8 + rows) % rows
    cell_col = first_cell % 128
    weights = cell_weight.transpose(1, 0, 2)
    received = lax.all_to_all(
        sent.reshape(nx * ny, 1, 128), ("gx", "gy"), 0, 0, tiled=True
    ).reshape(nx * ny, 128)
    pick, weight = call(
        cells_kernel,
        [((128, 1024), BF16), ((48, 1024), F32)],
        [cell_row, cell_col, weights],
        flops=1 << 28,
    )
    both, pick = lax.optimization_barrier((both, pick))
    first_low, first_high = with_neighbours(both, both, "gx")
    low_points, high_points = first_low[3:6], first_high[3:6]

    target, partial = call(
        near_own_kernel,
        [((8, 3, 128, 128), F32), ((8, 3, 128, 128), F32)],
        [near_counts, slots, points, slip],
        smem=2,
    )

    def near_field(whole, slip, low, high):
        args = [near_counts, slots, target, target if whole else partial]
        return call(
            functools.partial(near_rest_kernel, whole),
            [((3, 8, 128), F32)],
            [*args, points, low_points, high_points, slip, low, high],
            scratch=[
                pltpu.VMEM((3, 3, 8, 128), F32),
                pltpu.VMEM((3, 3, 8, 128), F32),
                pltpu.VMEM((8, 3, 128, 128), F32),
            ],
            smem=2,
            flops=1 << 28 if whole else 0,
        )[0]

    pieces = [pltpu.VMEM((16, 128), F32), pltpu.VMEM((16, 128), F32)]
    common = [strained, basis, normal_stress, friction, compliance, slip_state, dilation]
    common += [pick, weight]
    near = near_field(False, slip, first_low, first_high)
    slip, loaded, down, up, sent = call(
        first_update_kernel,
        [
            ((3, 8, 128), F32),
            ((24, 128), F32),
            ((6, 8, 128), F32),
            ((6, 8, 128), F32),
            ((nx, 16, 128), F32),
        ],
        [received, first_low, first_high, pressure, mobility, g_mat, h_mat, near, slip, *common],
        scratch=pieces,
    )
    received = lax.all_to_all(sent, "gx", 0, 0, tiled=True)
    low, high = with_neighbours(up, down, "gx")
    window, mobility_window, tile, sent = call(
        between_kernel,
        [((32, 128), F32), ((32, 128), F32), ((8, 128), F32), ((ny, 8, 128), F32)],
        [received, low, high, first_low, first_high, loaded, pressure, mobility],
    )
    received = lax.all_to_all(sent, "gy", 0, 0, tiled=True)
    near_slip, sent = lax.optimization_barrier((slip, sent))
    near = near_field(True, near_slip, low, high)
    slip, loaded, window, mobility_side, down, up, sent = call(
        second_update_kernel,
        [
            ((3, 8, 128), F32),
            ((24, 128), F32),
            ((32, 128), F32),
            ((32, 128), F32),
            ((2, 8, 128), F32),
            ((2, 8, 128), F32),
            ((nx, 8, 128), F32),
        ],
        [received, tile, window, mobility_window, h_mat, near, slip, *common],
        scratch=[pltpu.VMEM((8, 128), F32), pltpu.VMEM((8, 128), F32)],
    )
    received = lax.all_to_all(sent, "gx", 0, 0, tiled=True)
    low, high = with_neighbours(up, down, "gx")
    window, tile = call(
        last_kernel,
        [((32, 128), F32), ((8, 128), F32)],
        [received, low, high, loaded, window],
    )
    left = shift(tile, "gy", 1)
    right = shift(tile, "gy", -1)
    (final_pressure,) = call(
        final_kernel,
        [((8, 128), F32)],
        [window, left, right, mobility_window, mobility_side],
    )
    return (slip.transpose(1, 0, 2), final_pressure)


def solution(mesh):
    split = ("gy", "gx")
    in_specs = (
        P(split, None, None),
        P(split, None, None),
        P(split, None),
        P(split),
        P(split, None, None, None),
        P(),
        P(),
        P(split, None, None),
        P(split, None),
        P(split, None),
        P(split, None),
        P(split, None),
        P(split, None, None),
        P(split, None, None),
        P(split, None),
        P("gx", "gy"),
        P("gx", "gy"),
    )
    out_specs = (P(split, None, None), P("gx", "gy"))
    return jax.shard_map(shards, mesh=mesh, in_specs=in_specs, out_specs=out_specs, check_vma=False)
```

```python
import functools

import jax
import jax.numpy as jnp
from jax import lax
from jax.experimental import pallas as pl
from jax.experimental.pallas import tpu as pltpu
from jax.sharding import PartitionSpec as P

HI = lax.Precision.HIGHEST
F32 = jnp.float32
BF16 = jnp.bfloat16
SCALE = 0.04
SOFT = 0.25
LV = 9
RK = 16
GX_BITS = 5
HALO = 10

NN = (((1,), (0,)), ((), ()))
NT = (((1,), (1,)), ((), ()))
TN = (((0,), (0,)), ((), ()))


def dot(a, b, dims=NN, precision=HI):
    return lax.dot_general(a, b, dims, precision=precision, preferred_element_type=F32)


def iota(shape, dim):
    return lax.broadcasted_iota(jnp.int32, shape, dim)


def thirds(x):
    hi = x.astype(BF16)
    rest = x - hi.astype(F32)
    mid = rest.astype(BF16)
    low = (rest - mid.astype(F32)).astype(BF16)
    return jnp.concatenate([hi, mid, low], axis=0)


def split_lanes(x):
    hi = x.astype(BF16)
    rest = x - hi.astype(F32)
    mid = rest.astype(BF16)
    low = (rest - mid.astype(F32)).astype(BF16)
    return jnp.concatenate([hi, mid, low], axis=1)


def call(kernel, outs, args, scratch=(), smem=0, far=0, ends=(), flops=0, room=32):
    specs = [pl.BlockSpec(memory_space=pltpu.SMEM)] * smem
    specs += [pl.BlockSpec(memory_space=pl.ANY)] * far
    specs += [pl.BlockSpec(memory_space=pltpu.VMEM)] * (len(args) - smem - far)
    for at in ends:
        specs[at] = pl.BlockSpec((args[at].shape[0], 128), lambda i: (0, 7))
    return pl.pallas_call(
        kernel,
        out_shape=[jax.ShapeDtypeStruct(s, d) for s, d in outs],
        grid=(1,) if ends else (),
        in_specs=specs,
        out_specs=[pl.BlockSpec(memory_space=pltpu.VMEM)] * len(outs),
        scratch_shapes=list(scratch),
        compiler_params=pltpu.CompilerParams(vmem_limit_bytes=room * 1024 * 1024),
        cost_estimate=pl.CostEstimate(flops=flops, bytes_accessed=1 << 20, transcendentals=0),
    )(*args)


def setup_kernel(
    transfer,
    coupling,
    transfer_end,
    coupling_end,
    slip,
    basis,
    g_out,
    h_out,
    sent,
    held,
    sems,
):
    flat = lax.axis_index("gy") * lax.axis_size("gx") + lax.axis_index("gx")
    blocks = [pl.multiple_of(flat // 128 * 128, 128), pl.multiple_of(512 + flat // 256 * 128, 128)]
    blocks += [768, 896]
    copies = []
    for t, table in enumerate((transfer, coupling)):
        for b, start in enumerate(blocks[:3]):
            copies.append(
                pltpu.make_async_copy(
                    table.at[:, pl.ds(start, 128)], held.at[t, b], sems.at[t * 3 + b]
                )
            )
            copies[-1].start()
    total = jnp.zeros((RK, 128), F32)
    for c in range(8):
        for i in range(3):
            total += basis[c, i] * slip[i, c : c + 1, :]
    moment = dot(jnp.ones((8, 128), F32), total, NT)

    shape = (128, 256)
    level = iota(shape, 1) // RK
    first = 1024 - jnp.right_shift(jnp.full(shape, 1024, jnp.int32), level)
    wanted = first + jnp.right_shift(jnp.zeros(shape, jnp.int32) + flat, level)
    far_half = 1016 + 2 * jnp.bitwise_xor(flat // 256, 1) - LV
    wanted = jnp.where(level < LV, wanted, far_half + level)
    picks = []
    for b, start in enumerate(blocks):
        used = (level == b) if b < 3 else (level >= 3) & (level < LV + 2)
        pick = jnp.where((iota(shape, 0) + start == wanted) & used, 1.0, 0.0).astype(BF16)
        picks += [pick, pick, pick]
    picks = jnp.concatenate(picks, axis=0)
    mine = (iota((256, 256), 1) % RK) == (iota((256, 256), 0) // RK)
    inside = iota((256, 128), 1) < transfer.shape[1] - 896
    for copy in copies:
        copy.wait()

    def path_matrices(t, end):
        parts = [split_lanes(held[t, b]) for b in range(3)]
        parts.append(split_lanes(jnp.where(inside, end[...], 0.0)))
        spread = dot(jnp.concatenate(parts, axis=1), picks, NN, None)
        return jnp.sum(jnp.where(mine, spread, 0.0).reshape(RK, RK, 256), axis=0)

    lifts = path_matrices(0, transfer_end)
    across = path_matrices(1, coupling_end)
    chain = [lifts[:, l * RK : (l + 1) * RK] for l in range(LV - 1)]
    for apart in (1, 2, 4):
        chain = [
            chain[l] if l < apart else dot(chain[l], chain[l - apart]) for l in range(LV - 1)
        ]
    eye = jnp.where(iota((RK, RK), 0) == iota((RK, RK), 1), 1.0, 0.0).astype(F32)
    chain = [eye] + chain
    g_out[...] = jnp.zeros(g_out.shape, F32)
    h_out[...] = jnp.zeros(h_out.shape, F32)
    for l in range(LV):
        g_out[l * RK : (l + 1) * RK, :] = chain[l]
        h_out[l * RK : (l + 1) * RK, :] = dot(across[:, l * RK : (l + 1) * RK], chain[l])
    top = h_out[8 * RK : 9 * RK, :]
    for side in range(2):
        at = 256 + 128 * side + 7 * RK
        lane = (LV + side) * RK
        h_out[at : at + RK, :] = dot(lifts[:, lane : lane + RK], top, TN)
    low = dot(moment, g_out[0:128, :], NT)
    for p in range(sent.shape[0] // 8):
        sent[8 * p : 8 * p + 8, :] = low


def project(basis_ref, slip_rows, g_ref):
    total = jnp.zeros((RK, 128), F32)
    for c in range(8):
        for i in range(3):
            total += basis_ref[c, i] * slip_rows(i, c)
    moment = dot(jnp.ones((8, 128), F32), total, NT)
    return dot(moment, g_ref[0:128, :], NT), dot(moment, g_ref[128:256, :], NT)


def cells_kernel(row_in, col_in, weight, pick_out, weight_out):
    for c in range(8):
        lanes = slice(c * 128, (c + 1) * 128)
        row = row_in[c : c + 1, :]
        col = col_in[c : c + 1, :]
        pick_out[:, lanes] = jnp.where(iota((128, 128), 0) == col, 1.0, 0.0).astype(BF16)
        at = iota((24, 128), 0)
        for side in range(2):
            weight_out[side * 24 : side * 24 + 24, lanes] = jnp.where(
                at == row, weight[2 * side, c : c + 1, :], 0.0
            ) + jnp.where(at == row + 1, weight[2 * side + 1, c : c + 1, :], 0.0)


def add_pairs(counts, slots, target, total, points, slips, wanted):
    def one_target(c, _):
        def one_source(k, _):
            slot = slots[c, k]
            block = slot // 8
            row = pl.ds(slot % 8, 1)

            def add():
                y = [points(block)[i, row, :] for i in range(3)]
                s = [slips(block)[i, row, :] for i in range(3)]
                for part in range(8):
                    rows = slice(part * 16, part * 16 + 16)
                    r = [target[c, i, rows, :] - y[i] for i in range(3)]
                    inverse = lax.rsqrt(r[0] * r[0] + r[1] * r[1] + r[2] * r[2] + SOFT)
                    along = (r[0] * s[0] + r[1] * s[1] + r[2] * s[2]) * (inverse * inverse)
                    for i in range(3):
                        total[c, i, rows, :] += inverse * (s[i] + along * r[i])

            if wanted is None:
                add()
            else:
                pl.when(wanted(block))(add)
            return 0

        return lax.fori_loop(0, counts[c], one_source, 0)

    lax.fori_loop(0, 8, one_target, 0)


def near_own_kernel(counts, slots, own_points, own, target, total):
    ones = jnp.ones((384, 128), BF16)
    diagonal = iota((128, 128), 0) == iota((128, 128), 1)
    for c in range(8):
        for i in range(3):
            wide = jnp.where(diagonal, own_points[i, c : c + 1, :], 0.0)
            target[c, i] = dot(split_lanes(wide), ones, NN, None)
    total[...] = jnp.zeros(total.shape, F32)
    add_pairs(counts, slots, target, total, lambda b: own_points, lambda b: own, lambda b: b == 1)


def near_rest_kernel(whole, counts, slots, target, partial, *refs):
    (own_points, low_points, high_points, own, low, high, near_out, points, slips, total) = refs
    for b, (p, s) in enumerate(((low_points, low), (own_points, own), (high_points, high))):
        for i in range(3):
            points[b, i] = p[i]
            slips[b, i] = s[i]
    total[...] = jnp.zeros(total.shape, F32) if whole else partial[...]
    wanted = None if whole else lambda b: b != 1
    add_pairs(counts, slots, target, total, lambda b: points.at[b], lambda b: slips.at[b], wanted)
    ones = jnp.ones((384, 128), BF16)
    diagonal = iota((128, 128), 0) == iota((128, 128), 1)
    for c in range(8):
        for i in range(3):
            summed = dot(split_lanes(total[c, i]), ones, NN, None)
            near_out[i, c : c + 1, :] = SCALE * jnp.sum(
                jnp.where(diagonal, summed, 0.0), axis=0, keepdims=True
            )


def pack_kernel(after, slip, points, pressure, mobility, out):
    out[0:3] = slip[...]
    out[3:6] = points[...]
    out[6] = pressure[...]
    out[7] = mobility[...]


def pick_edges(window):
    row, lane = iota((8, 128), 0), iota((8, 128), 1)
    wanted = jnp.where(row < 2, row, row + 124)
    pick = jnp.where((lane == wanted) & (row < 4), 1.0, 0.0).astype(F32)
    return dot(pick, window, NT)


def sum_over_row(received, at, first):
    j = lax.axis_index("gx")
    row, lane = iota((8, 128), 0), iota((8, 128), 1)
    level = lane // RK + jnp.where(row == first + 1, 8, 0)
    own = jnp.right_shift(jnp.zeros((8, 128), jnp.int32) + j, level)
    total = jnp.zeros((8, 128), F32)
    for p in range(received.shape[0]):
        theirs = jnp.right_shift(jnp.full((8, 128), p, jnp.int32), level)
        used = (level >= GX_BITS) | (theirs == jnp.bitwise_xor(own, 1))
        total += jnp.where(used, received[p, at : at + 8, :], 0.0)
    return total


def copies_of(tile, sent):
    for p in range(sent.shape[0]):
        sent[p] = tile[...]


def between_kernel(
    received,
    low,
    high,
    first_low,
    first_high,
    loaded,
    pressure,
    mobility,
    window,
    mobility_out,
    tile_out,
    sent,
):
    j = lax.axis_index("gx")
    peers = received.shape[0]
    before = lax.rem(j - 2 + peers, peers)
    after = lax.rem(j + 2, peers)
    for out, own, at in ((window, pressure, 6), (mobility_out, mobility, 7)):
        out[...] = jnp.zeros(out.shape, F32)
        out[2:10, :] = first_low[at]
        out[10:18, :] = own[...]
        out[18:26, :] = first_high[at]
    mobility_out[1:2, :] = received[before, 12:13, :]
    mobility_out[26:27, :] = received[after, 12:13, :]
    window[2:26, :] += loaded[...]
    for i, at, size in ((3, 0, 8), (4, 8, 8), (5, 16, 2)):
        window[at : at + size, :] += low[i, 0:size, :]
        window[at + 10 : at + 10 + size, :] += high[i, 0:size, :]
    window[18:28, :] += received[after, 0:10, :]
    window[0:10, :] += received[before, 0:10, :]
    window[26:28, :] += received[lax.rem(j + 3, peers), 0:2, :]
    window[0:2, :] += received[lax.rem(j - 3 + peers, peers), 8:10, :]
    sums = sum_over_row(received, 8, 2)
    tile_out[...] = jnp.zeros(tile_out.shape, F32)
    edges = pick_edges(window[...])
    tile_out[0:4, 0:32] = edges[0:4]
    tile_out[4:6, :] = sums[2:4]
    edges = pick_edges(mobility_out[...])
    tile_out[6:7, 0:32] = edges[0:1]
    tile_out[7:8, 0:32] = edges[3:4]
    copies_of(tile_out, sent)


def last_kernel(first, second, third, loaded, pressure, window, tile_out):
    even = lax.rem(lax.axis_index("gx"), 2) == 0
    window[...] = pressure[...]
    window[2:26, :] += loaded[...]
    for i, size in ((0, 8), (1, 2)):
        one, two = first[i, 0:size, :], second[i, 0:size, :]
        window[8 + 8 * i : 8 + 8 * i + size, :] += jnp.where(even, two, one)
        window[10 + 8 * i : 10 + 8 * i + size, :] += jnp.where(even, one, two)
    relayed, last = second[1, 2:4, :], third[0:2, :]
    window[8:10, :] += jnp.where(even, relayed, last)
    window[18:20, :] += jnp.where(even, last, relayed)
    tile_out[...] = jnp.zeros(tile_out.shape, F32)
    tile_out[0:4, 0:32] = pick_edges(window[...])[0:4]


def beside(left, right):
    g = lax.axis_index("gy")
    row, lane = iota((8, 128), 0), iota((8, 128), 1)
    from_right = (row < 2) | (row == 6)
    inside = (from_right & (g < lax.axis_size("gy") - 1)) | (~from_right & (g > 0))
    edges = jnp.where(inside, jnp.where(from_right, right, left), 0.0)[:, 0:32]
    wanted = jnp.where(row < 2, row, row + 124)
    pick = jnp.where((lane == wanted) & (row < 4), 1.0, 0.0).astype(F32)
    wanted = jnp.where(row == 6, 0, 127)
    pick_mobility = jnp.where((lane == wanted) & (row > 5), 1.0, 0.0).astype(F32)
    return dot(edges, pick, TN), dot(edges, pick_mobility, TN)


def flow(window, window_side, mobility, mobility_side):
    j = lax.axis_index("gx")
    p = jnp.concatenate([window, window_side], axis=1)
    m = jnp.concatenate([mobility, mobility_side], axis=1)
    rows = 8 * lax.axis_size("gx")
    row = lax.rem(iota((32, 256), 0) + (j * 8 - HALO + rows), jnp.full((32, 256), 0, jnp.int32) + rows)
    for step in range(2):
        up = jnp.where(row == 0, 0.0, pltpu.roll(p, 1, 0))
        down = jnp.where(row == rows - 1, 0.0, pltpu.roll(p, 31, 0))
        sides = pltpu.roll(p, 1, 1) + pltpu.roll(p, 255, 1)
        p = p + m * (up + down + sides - 4.0 * p)
    return p[:, 0:128]


def incoming_of_row(received, tile, h):
    g = lax.axis_index("gy")
    row, lane = iota((8, 128), 0), iota((8, 128), 1)
    level = lane // RK + jnp.where(row == 5, 8, 0)
    bit = jnp.maximum(level - GX_BITS, 0)
    own = jnp.right_shift(jnp.zeros((8, 128), jnp.int32) + g, bit)
    total = jnp.where((level < GX_BITS) & (row == 4), tile[...], 0.0)
    within = (level >= GX_BITS) & (level < LV) & ((row == 4) | (row == 5))
    for p in range(received.shape[0]):
        theirs = jnp.right_shift(jnp.full((8, 128), p, jnp.int32), bit)
        total += jnp.where(within & (theirs == jnp.bitwise_xor(own, 1)), received[p], 0.0)
    parts = jnp.where(iota((8, RK), 0) == 4, dot(total, h[0:128, :]), 0.0)
    return parts + jnp.where(iota((8, RK), 0) == 5, dot(total, h[128:256, :]), 0.0)


def incoming_of_all(received, h):
    ny = lax.axis_size("gy")
    flat = lax.axis_index("gy") * lax.axis_size("gx") + lax.axis_index("gx")
    row, level = iota((8, 128), 0), iota((8, 128), 1) // RK
    sibling = jnp.bitwise_xor(jnp.right_shift(jnp.zeros((8, 128), jnp.int32) + flat, level), 1)
    half = jnp.bitwise_xor(flat // 256, 1)
    sums = [jnp.zeros((8, 128), F32) for _ in range(3)]
    for at in range(0, received.shape[0], 8):
        theirs = received[at : at + 8, :]
        node = (at % ny + row) * lax.axis_size("gx") + at // ny
        upper = jnp.right_shift(node, 7)
        sums[0] += jnp.where(jnp.right_shift(node, level) == sibling, theirs, 0.0)
        sums[1] += jnp.where(upper == 2 * half, theirs, 0.0)
        sums[2] += jnp.where(upper == 2 * half + 1, theirs, 0.0)
    parts = dot(sums[0], h[0:128, :]) + dot(sums[1], h[256:384, :])
    return parts + dot(sums[2], h[384:512, :])


def update(parts, cells, near, refs, slip_out, loaded_out):
    (slip, prestress, basis, normal, friction, compliance, state, dilation, pick, weight) = refs
    incoming = dot(parts, jnp.ones((8, 128), F32), TN)

    both = jnp.concatenate([cells, pltpu.roll(cells, 127, 1)], axis=0)
    split = thirds(both)
    found = dot(split, pick[...], NN, None)
    found = (found[0:48] + found[48:96] + found[96:144]) * weight[...]
    at_row = jnp.sum(found, axis=0, keepdims=True)

    for c in range(8):
        for i in range(3):
            far = jnp.sum(basis[c, i] * incoming, axis=0, keepdims=True)
            slip_out[i, c : c + 1, :] = far
    at_elements = jnp.concatenate([at_row[:, c * 128 : (c + 1) * 128] for c in range(8)], axis=0)
    stress = [prestress[i] - (near[i] + slip_out[i]) for i in range(3)]
    effective = normal[...] - at_elements
    magnitude = jnp.sqrt(stress[0] * stress[0] + stress[1] * stress[1] + stress[2] * stress[2] + 1.0)
    factor = jnp.maximum(1.0 - friction[...] * effective / magnitude, 0.0)
    scaled = state[...].astype(F32) * compliance[...] * factor
    steps = [scaled * stress[i] for i in range(3)]
    for i in range(3):
        slip_out[i] = slip[i] + steps[i]
    dilated = dilation[...] * (steps[0] * steps[0] + steps[1] * steps[1] + steps[2] * steps[2])
    dilated_row = jnp.concatenate([dilated[c : c + 1, :] for c in range(8)], axis=1)
    spread = dot(thirds(weight[...] * dilated_row), pick[...], NT, None)
    spread = spread[0:48] + spread[48:96] + spread[96:144]
    loaded_out[...] = spread[0:24] + pltpu.roll(spread[24:48], 1, 1)


def send_sources(ahead, behind, sent):
    j = lax.axis_index("gx")
    peers = sent.shape[0]
    for p in range(peers):
        back = lax.rem(j - p + peers, peers) < peers // 2
        sent[p] = jnp.where(back, ahead[...], behind[...])


def first_update_kernel(received, low, high, pressure, mobility, lifts, h, near, *refs):
    refs, outs = refs[:10], refs[10:]
    slip_out, loaded, down_out, up_out, sent, ahead, behind = outs
    cells = jnp.concatenate([low[6], pressure[...], high[6]], axis=0)
    update(incoming_of_all(received, h), cells, near, refs, slip_out, loaded)
    low_row, high_row = project(refs[2], lambda i, c: slip_out[i, c : c + 1, :], lifts)
    ahead[...] = jnp.zeros(ahead.shape, F32)
    behind[...] = jnp.zeros(behind.shape, F32)
    ahead[0:10, :] = loaded[0:10, :]
    behind[0:10, :] = loaded[14:24, :]
    ahead[8:10, :] += pressure[0:2, :]
    behind[0:2, :] += pressure[6:8, :]
    ahead[12:13, :] = mobility[0:1, :]
    behind[12:13, :] = mobility[7:8, :]
    for out in (ahead, behind):
        out[10:11, :] = low_row[0:1]
        out[11:12, :] = high_row[0:1]
    send_sources(ahead, behind, sent)
    for out, at in ((down_out, 0), (up_out, 6)):
        out[0:3] = slip_out[...]
        out[3] = loaded[at : at + 8, :]
        out[4] = loaded[at + 8 : at + 16, :]
        out[5] = jnp.zeros((8, 128), F32)
        out[5, 0:2, :] = loaded[at + 16 : at + 18, :]


def second_update_kernel(received, tile, window, mobility, h, near, *refs):
    refs, outs = refs[:10], refs[10:]
    slip_out, loaded, window_out, side_out, down_out, up_out = outs
    g = lax.axis_index("gy")
    left = received[jnp.maximum(g - 1, 0)]
    right = received[jnp.minimum(g + 1, received.shape[0] - 1)]
    side, mobility_side = beside(left, right)
    side_out[...] = mobility_side
    window_out[...] = flow(window[...], side, mobility[...], mobility_side)
    parts = incoming_of_row(received, tile, h)
    update(parts, window_out[2:26, :], near, refs, slip_out, loaded)
    for out, at in ((down_out, 0), (up_out, 14)):
        out[0] = loaded[at : at + 8, :]
        out[1] = jnp.zeros((8, 128), F32)
        out[1, 0:2, :] = loaded[at + 8 : at + 10, :]


def final_kernel(window, left, right, mobility, mobility_side, out):
    side, _ = beside(left[...], right[...])
    done = flow(window[...], side, mobility[...], mobility_side[...])
    out[...] = done[HALO : HALO + 8, :]


def shift(x, axis, steps):
    n = lax.axis_size(axis)
    return lax.ppermute(x, axis, [(i, (i + steps) % n) for i in range(n)])


def with_neighbours(up, down, axis):
    n = lax.axis_size(axis)
    even = lax.axis_index(axis) % 2 == 0
    alike = up is down
    first = up if alike else jnp.where(even, up, down)
    second = up if alike else jnp.where(even, down, up)
    first = lax.ppermute(first, axis, [(i, i ^ 1) for i in range(n)])
    second = lax.ppermute(second, axis, [(i, (i + 2 * (i % 2) - 1) % n) for i in range(n)])
    return jnp.where(even, second, first), jnp.where(even, first, second)


def relayed_along_gx(up, down):
    n = lax.axis_size("gx")
    even = lax.axis_index("gx") % 2 == 0
    near_pairs = [(i, i ^ 1) for i in range(n)]
    first = lax.ppermute(jnp.where(even, up, down), "gx", near_pairs)
    own = jnp.where(even, down, up)
    relay = jnp.where(even, first[0, 0:2], first[1, 0:2])
    tail = jnp.concatenate([own[1, 0:2], relay, own[1, 4:8]], axis=0)
    pairs = [(i, (i + 2 * (i % 2) - 1) % n) for i in range(n)]
    second = lax.ppermute(jnp.stack([own[0], tail]), "gx", pairs)
    third = lax.ppermute(jnp.where(even, second[1], second[0]), "gx", near_pairs)
    return first, second, third


def shards(
    slip_field,
    positions,
    neighbours,
    near_counts,
    cluster_basis,
    transfer,
    coupling,
    prestress,
    normal_stress,
    friction,
    compliance,
    slip_state,
    cell_index,
    cell_weight,
    dilation,
    pressure,
    mobility,
):
    nx, ny = lax.axis_size("gx"), lax.axis_size("gy")
    j, g = lax.axis_index("gx"), lax.axis_index("gy")
    rows = 8 * nx
    slip = slip_field.transpose(1, 0, 2)
    points = positions.transpose(1, 0, 2)
    strained = prestress.transpose(1, 0, 2)
    basis = cluster_basis.transpose(0, 2, 1, 3)
    lift_table = transfer.transpose(1, 2, 0).reshape(RK * RK, -1)
    cross_table = coupling.transpose(1, 2, 0).reshape(RK * RK, -1)
    slots = (neighbours - j * 8 + 8 + rows) % rows

    g_mat, h_mat, sent = call(
        setup_kernel,
        [((256, RK), F32), ((512, RK), F32), ((nx * ny, 128), F32)],
        [lift_table, cross_table, lift_table, cross_table, slip, basis],
        scratch=[pltpu.VMEM((2, 3, 256, 128), F32), pltpu.SemaphoreType.DMA((6,))],
        far=2,
        ends=(2, 3),
        room=60,
    )
    (both,) = call(
        pack_kernel,
        [((8, 8, 128), F32)],
        [h_mat, slip, points, pressure, mobility],
        far=1,
        flops=1 << 28,
    )
    sent, cell_index, cell_weight = lax.optimization_barrier((sent, cell_index, cell_weight))
    first_cell = cell_index[:, 0, :]
    cell_row = (first_cell // 128 - j * 8 + 8 + rows) % rows
    cell_col = first_cell % 128
    weights = cell_weight.transpose(1, 0, 2)
    received = lax.all_to_all(
        sent.reshape(nx * ny, 1, 128), ("gx", "gy"), 0, 0, tiled=True
    ).reshape(nx * ny, 128)
    pick, weight = call(
        cells_kernel,
        [((128, 1024), BF16), ((48, 1024), F32)],
        [cell_row, cell_col, weights],
        flops=1 << 28,
    )
    both, pick = lax.optimization_barrier((both, pick))
    first_low, first_high = with_neighbours(both, both, "gx")
    low_points, high_points = first_low[3:6], first_high[3:6]

    target, partial = call(
        near_own_kernel,
        [((8, 3, 128, 128), F32), ((8, 3, 128, 128), F32)],
        [near_counts, slots, points, slip],
        smem=2,
    )

    def near_field(whole, slip, low, high):
        args = [near_counts, slots, target, target if whole else partial]
        return call(
            functools.partial(near_rest_kernel, whole),
            [((3, 8, 128), F32)],
            [*args, points, low_points, high_points, slip, low, high],
            scratch=[
                pltpu.VMEM((3, 3, 8, 128), F32),
                pltpu.VMEM((3, 3, 8, 128), F32),
                pltpu.VMEM((8, 3, 128, 128), F32),
            ],
            smem=2,
            flops=1 << 28 if whole else 0,
        )[0]

    pieces = [pltpu.VMEM((16, 128), F32), pltpu.VMEM((16, 128), F32)]
    common = [strained, basis, normal_stress, friction, compliance, slip_state, dilation]
    common += [pick, weight]
    near = near_field(False, slip, first_low, first_high)
    slip, loaded, down, up, sent = call(
        first_update_kernel,
        [
            ((3, 8, 128), F32),
            ((24, 128), F32),
            ((6, 8, 128), F32),
            ((6, 8, 128), F32),
            ((nx, 16, 128), F32),
        ],
        [received, first_low, first_high, pressure, mobility, g_mat, h_mat, near, slip, *common],
        scratch=pieces,
    )
    received = lax.all_to_all(sent, "gx", 0, 0, tiled=True)
    low, high = with_neighbours(up, down, "gx")
    window, mobility_window, tile, sent = call(
        between_kernel,
        [((32, 128), F32), ((32, 128), F32), ((8, 128), F32), ((ny, 8, 128), F32)],
        [received, low, high, first_low, first_high, loaded, pressure, mobility],
    )
    received = lax.all_to_all(sent, "gy", 0, 0, tiled=True)
    near_slip, sent = lax.optimization_barrier((slip, sent))
    near = near_field(True, near_slip, low, high)
    slip, loaded, window, mobility_side, down, up = call(
        second_update_kernel,
        [
            ((3, 8, 128), F32),
            ((24, 128), F32),
            ((32, 128), F32),
            ((32, 128), F32),
            ((2, 8, 128), F32),
            ((2, 8, 128), F32),
        ],
        [received, tile, window, mobility_window, h_mat, near, slip, *common],
    )
    first, second, third = relayed_along_gx(up, down)
    window, tile = call(
        last_kernel,
        [((32, 128), F32), ((8, 128), F32)],
        [first, second, third, loaded, window],
    )
    left = shift(tile, "gy", 1)
    right = shift(tile, "gy", -1)
    (final_pressure,) = call(
        final_kernel,
        [((8, 128), F32)],
        [window, left, right, mobility_window, mobility_side],
    )
    return (slip.transpose(1, 0, 2), final_pressure)


def solution(mesh):
    split = ("gy", "gx")
    in_specs = (
        P(split, None, None),
        P(split, None, None),
        P(split, None),
        P(split),
        P(split, None, None, None),
        P(),
        P(),
        P(split, None, None),
        P(split, None),
        P(split, None),
        P(split, None),
        P(split, None),
        P(split, None, None),
        P(split, None, None),
        P(split, None),
        P("gx", "gy"),
        P("gx", "gy"),
    )
    out_specs = (P(split, None, None), P("gx", "gy"))
    return jax.shard_map(shards, mesh=mesh, in_specs=in_specs, out_specs=out_specs, check_vma=False)
```
